128 devices in a mesh: row: 16 (over z, y_lo, core), col: 8 (over x, y_hi).
Axes of the slice: x: 4, y: 4 (y_hi: 2, y_lo: 2; y = y_hi * 2 + y_lo), z: 4, core: 2. Of those that a mesh axis runs over, the one named last changes fastest.
Arguments:
- query_proj: float32 [2048, 80, 128], P('col', 'row'), may hold values from -6 to 6
- key_proj: float32 [2048, 80, 128], P('col', 'row'), may hold values from -6 to 6
- value_proj: float32 [2048, 80, 128], P('col', 'row'), may hold values from -6 to 6
- out_grad: float32 [2048, 80, 128], P('col', 'row'), may hold values from -12 to 12
- pair_bias: float32 [4, 2048, 2048], P(None, 'row', 'col'), may hold values from -6 to 6
- log_sum_exp: float32 [4, 80, 2048], P(None, 'row', 'col'), as said below
- correction: float32 [4, 80, 2048], P(None, 'row', 'col'), may hold values from -12 to 12
- pad_mask: int32 [2048], replicated, may hold values from 0 to 1, as said below
Outputs:
- grad_query: float32 [2048, 80, 128], P('col', 'row')
- grad_key: float32 [2048, 80, 128], P('col', 'row')
- grad_value: float32 [2048, 80, 128], P('col', 'row')
- grad_bias: float32 [4, 2048, 2048], P(None, 'row', 'col')
The draws below stay inside these ranges and needn't reach their ends.
Inputs may be any that keep to these rules, and one draw needn't show every extreme that they name: `pad_mask`: token 0 is always a real residue, about one token in eight is padding. `log_sum_exp`: each entry lies between log(2048) + 1 and log(2048) + 3.5.
All inputs are finite; a program needn't handle non-finite values.
Results may differ from the reference program's by a relative error of at most 0.0003.
Values sent between devices are 32-bit elements; how exact they have to be, the bound alone decides.
A program may use at most 128 MiB of HBM per device.

```python
import math
import jax
import jax.numpy as jnp
from jax import lax

C = 128
H = 4
DH = 32
N = 2048
SLAB = 80


def draw_pad_mask(key, part):
    alive_keys = (jax.random.randint(key, (N,), 0, 8) > 0).astype(jnp.int32)
    return alive_keys.at[0].set(1)


def draw_log_sum_exp(key, part):
    base_level = math.log(N) + 1.0
    spread = jax.random.uniform(key, (H, SLAB, N), jnp.float32, 0.0, 1.5)
    return (base_level + spread).astype(jnp.float32)


def shard_levels(key, shape, split, least, top_value):
    def one(position, blocks):
        draws = jax.random.uniform(jax.random.fold_in(jax.random.fold_in(key, 6), position), (blocks,), jnp.float32, least / len(split), top_value / len(split))
        return jnp.repeat(jnp.exp(draws), shape[position] // blocks).reshape((-1,) + (1,) * (len(shape) - position - 1))

    factor_of = one(*split[0])
    for cut in split[1:]:
        factor_of = factor_of * one(*cut)
    return factor_of


def noise(own_key, extent, deviation, limit, split=(), kind=jnp.bfloat16):
    factor_of = shard_levels(own_key, extent, split, -0.22, 0.18) if split else 1.0
    drawn = jax.random.normal(own_key, extent, jnp.float32) * deviation * factor_of
    return jnp.minimum(jnp.maximum(drawn, -limit), limit).astype(kind)


def setup_inputs(seed: int = 0) -> dict:
    splits = jax.random.split(jax.random.key(seed), 9)
    return {
        "query_proj": noise(splits[0], (N, SLAB, C), 1.0, 6.0, ((0, 8), (1, 16)), jnp.float32),
        "key_proj": noise(splits[1], (N, SLAB, C), 1.0, 6.0, ((0, 8), (1, 16)), jnp.float32),
        "value_proj": noise(splits[2], (N, SLAB, C), 1.0, 6.0, ((0, 8), (1, 16)), jnp.float32),
        "out_grad": noise(splits[3], (N, SLAB, C), 2.0, 12.0, ((0, 8), (1, 16)), jnp.float32),
        "pair_bias": noise(splits[4], (H, N, N), 1.0, 6.0, ((1, 16), (2, 8)), jnp.float32),
        "log_sum_exp": draw_log_sum_exp(jax.random.fold_in(splits[8], 71), 0),
        "correction": noise(splits[6], (H, SLAB, N), 2.0, 12.0, ((1, 16), (2, 8)), jnp.float32),
        "pad_mask": draw_pad_mask(jax.random.fold_in(splits[8], 71), 0),
    }


def reference(query_proj, key_proj, value_proj, out_grad, pair_bias, log_sum_exp, correction, pad_mask):
    highest = lax.Precision.HIGHEST
    inv_root = 1.0 / math.sqrt(DH)
    alive_keys = pad_mask == 1
    query_cols = jnp.transpose(query_proj, (1, 0, 2)).reshape(SLAB, N, H, DH)
    key_cols = jnp.transpose(key_proj, (1, 0, 2)).reshape(SLAB, N, H, DH)
    value_cols = jnp.transpose(value_proj, (1, 0, 2)).reshape(SLAB, N, H, DH)
    grad_cols = jnp.transpose(out_grad, (1, 0, 2)).reshape(SLAB, N, H, DH)
    lse_cols = jnp.transpose(log_sum_exp, (1, 0, 2))
    corr_cols = jnp.transpose(correction, (1, 0, 2))
    bias_turned = jnp.transpose(pair_bias, (0, 2, 1))

    def column_step(bias_total, column_data):
        query_col, key_col, value_col, grad_col, lse_col, corr_col = column_data
        scores = jnp.einsum('ihd,khd->hik', query_col, key_col, precision=highest) * inv_root + bias_turned
        softmax_w = jnp.where(alive_keys[None, None, :], jnp.exp(scores - lse_col[:, :, None]), jnp.float32(0.0))
        prob_grad = jnp.einsum('ihd,khd->hik', grad_col, value_col, precision=highest)
        score_grad = softmax_w * (prob_grad - corr_col[:, :, None])
        query_grad = jnp.einsum('hik,khd->ihd', score_grad, key_col, precision=highest) * inv_root
        key_grad = jnp.einsum('hik,ihd->khd', score_grad, query_col, precision=highest) * inv_root
        value_grad = jnp.einsum('hik,ihd->khd', softmax_w, grad_col, precision=highest)
        return (bias_total + score_grad, (query_grad, key_grad, value_grad))
    bias_start = jnp.zeros((H, N, N), jnp.float32)
    bias_total, column_grads = lax.scan(column_step, bias_start, (query_cols, key_cols, value_cols, grad_cols, lse_cols, corr_cols))
    query_grad, key_grad, value_grad = column_grads

    def back_shape(stacked):
        return jnp.transpose(stacked.reshape(SLAB, N, C), (1, 0, 2))
    grad_bias = jnp.transpose(bias_total, (0, 2, 1))
    return (back_shape(query_grad), back_shape(key_grad), back_shape(value_grad), grad_bias)
```

```python
import functools
import math

import jax
import jax.numpy as jnp
from jax import lax
from jax.experimental import pallas as pl
from jax.experimental.pallas import tpu as pltpu
from jax.sharding import PartitionSpec as P

LOG2E = math.log2(math.e)
ROOT = 1.0 / math.sqrt(32)
BF = jnp.bfloat16
F32 = jnp.float32
MESH = pl.DeviceIdType.MESH


def place(z, a, k, x, b):
    return (z * 4 + a * 2 + k, x * 2 + b)


def dg(lhs, rhs, lhs_dim, rhs_dim):
    return lax.dot_general(
        lhs, rhs, (((lhs_dim,), (rhs_dim,)), ((), ())), preferred_element_type=F32
    )


def split(x):
    hi = x.astype(BF)
    return hi, (x - hi.astype(F32)).astype(BF)


def extra_rows(x):
    hi = x.astype(BF)
    rest = x - hi.astype(F32)
    mid = rest.astype(BF)
    low = (rest - mid.astype(F32)).astype(BF)
    row = lax.broadcasted_iota(jnp.int32, (32, x.shape[1]), 0)
    out = jnp.where(
        row == 0,
        hi.astype(F32),
        jnp.where(row == 1, mid.astype(F32), jnp.where(row == 2, low.astype(F32), 0.0)),
    )
    return out.astype(BF)


def key_rows(x):
    hi, low = split(x)
    ones = jnp.ones((32, x.shape[1]), BF)
    return hi, low, jnp.concatenate([hi, low, hi, ones], axis=0)


def pack_queries(half, qgb, lrb, qp, gp):
    cols = slice(256 * half, 256 * half + 256)

    def step(t, carry):
        src = t // 5
        j = t % 5
        for h in range(2):
            rows = slice(32 * h, 32 * h + 32)
            level = lrb[half, src, 0, h, pl.ds(j, 1), :] * (-LOG2E)
            corr = -lrb[half, src, 1, h, pl.ds(j, 1), :]
            for which, packed, scale, row in ((0, qp, LOG2E * ROOT, level), (1, gp, None, corr)):
                x = qgb[half, src, which, j, rows, :]
                hi, low = split(x if scale is None else x * scale)
                packed[src, j, h, 0:32, cols] = hi
                packed[src, j, h, 32:64, cols] = hi
                packed[src, j, h, 64:96, cols] = low
                packed[src, j, h, 96:128, cols] = extra_rows(row)
        return carry

    lax.fori_loop(0, 10, step, 0)


def compute_block(kv, qp, gp, bias, dkv, dqb, db, scr, first):
    for half in range(2):
        for part in range(2):
            for h in range(2):
                db[half, part, h] = jnp.zeros((128, 256), F32)

    def step(t, carry):
        src = t // 5
        j = t % 5
        for h in range(2):
            w_hi, w_low, s_hi, s_low = [scr.at[h, i] for i in range(4)]
            rows = slice(32 * h, 32 * h + 32)
            k_hi, k_low, kp = key_rows(kv[src, 0, j, rows, :])
            _, _, vp = key_rows(kv[src, 1, j, rows, :])
            for half in range(2):
                cols = slice(256 * half, 256 * half + 256)
                st = dg(kp, qp[src, j, h, :, cols], 0, 0)
                pt = dg(vp, gp[src, j, h, :, cols], 0, 0)
                for part in range(2):
                    keys = slice(128 * part, 128 * part + 128)
                    w = jnp.exp2(st[keys] + bias[half, part, h])
                    ds = w * pt[keys]
                    db[half, part, h] += ds
                    w_hi[keys, cols], w_low[keys, cols] = split(w)
                    s_hi[keys, cols], s_low[keys, cols] = split(ds)
            k2 = jnp.concatenate([k_hi, k_low], axis=0)
            r = dg(k2, s_hi[...], 1, 0)
            total = (r[:32] + r[32:] + dg(k_hi, s_low[...], 1, 0)) * ROOT
            for half in range(2):
                mine = total[:, 256 * half : 256 * half + 256]
                dqb[half, src, j, rows, :] = jnp.where(first, mine, dqb[half, src, j, rows, :] + mine)
            r = dg(qp[src, j, h, 32:96, :], s_hi[...], 1, 1)
            r2 = dg(qp[src, j, h, 0:32, :], s_low[...], 1, 1)
            dkv[src, 0, j, rows, :] = (r[:32] + r[32:] + r2) * (1.0 / LOG2E)
            r = dg(gp[src, j, h, 32:96, :], w_hi[...], 1, 1)
            r2 = dg(gp[src, j, h, 0:32, :], w_low[...], 1, 1)
            dkv[src, 1, j, rows, :] = r[:32] + r[32:] + r2
        return carry

    lax.fori_loop(0, 10, step, 0)


def kernel(
    q_ref, k_ref, v_ref, g_ref, b_ref, l_ref, r_ref, m_ref,
    dq_ref, dk_ref, dv_ref, db_ref,
    skv, sqg, sbb, slr, kvb, qgb, lrb, bb, dkv, rkv, dqb, rdq, dbb, rb, rbb, qp, gp, scr,
    kvs, kvr, qgs, qgr, lrs, lrr, b1s, b1r, b2s, b2r, dks, dkr, dqs, dqr, dbs, dbr, d1s, d1r,
):
    row = lax.axis_index("row")
    col = lax.axis_index("col")
    z = row // 4
    a = (row // 2) % 2
    k = row % 2
    x = col // 2
    b = col % 2

    def at(dz=0, dx=0, dk=0):
        return place((z + dz) % 4, a, (k + dk) % 2, (x + dx) % 4, b)

    barrier = pltpu.get_barrier_semaphore()
    partners = [at(dx=dx, dk=dk) for dx in (1, 2, 3) for dk in (0, 1)]
    partners += [at(dz=dz) for dz in (1, 2, 3)]
    for da in (0, 1):
        for dy in (0, 1):
            for dk in (0, 1):
                if da or dy or dk:
                    partners.append(place(z, (a + da) % 2, (k + dk) % 2, x, (b + dy) % 2))
    for partner in partners:
        pl.semaphore_signal(barrier, inc=1, device_id=partner, device_id_type=MESH)

    def remote(src, dst, send, recv, target):
        return pltpu.make_async_remote_copy(
            src_ref=src, dst_ref=dst, send_sem=send, recv_sem=recv,
            device_id=target, device_id_type=MESH,
        )

    def done(ref, sem):
        pltpu.make_async_copy(ref, ref, sem).wait()

    def turn(ref, dst, which):
        for j in range(5):
            t = ref[:, j, :].T
            dst[0, which, j] = t[:64]
            dst[1, which, j] = t[64:]

    alive = jnp.broadcast_to(m_ref[pl.ds(row, 1), :], (128, 128)).astype(F32).T
    alive = jnp.concatenate([alive, alive], axis=1) == 1.0
    for h in range(4):
        sbb[h // 2, h % 2] = jnp.where(alive, b_ref[h] * LOG2E, -1e30)
    for d in range(2):
        for h in range(2):
            slr[d, 0, h] = l_ref[2 * d + h]
            slr[d, 1, h] = r_ref[2 * d + h]

    pl.semaphore_wait(barrier, len(partners))

    for da in (0, 1):
        for dk in (0, 1):
            a_to = (a + da) % 2
            d = (k + dk) % 2
            copy = remote(
                sbb.at[d], bb.at[z, b, k], b1s.at[da, dk], b1r.at[b, k], place(z, a_to, d, x, a)
            )
            if da == 0 and dk == 0:
                pl.when(a == b)(
                    lambda: pltpu.make_async_copy(sbb.at[k], bb.at[z, b, k], b1r.at[b, k]).start()
                )
                pl.when(a != b)(copy.start)
            else:
                copy.start()

    turn(k_ref, skv, 0)
    turn(v_ref, skv, 1)
    pltpu.make_async_copy(skv.at[k], kvb.at[x, k], kvr.at[x, k]).start()
    for dx, dk in ((0, 1), (1, 0), (3, 0), (1, 1), (3, 1), (2, 0), (2, 1)):
        remote(
            skv.at[(k + dk) % 2], kvb.at[x, k], kvs.at[dx, dk], kvr.at[x, k], at(dx=dx, dk=dk)
        ).start()

    turn(q_ref, sqg, 0)
    turn(g_ref, sqg, 1)
    pltpu.make_async_copy(sqg.at[k], qgb.at[b, k], qgr.at[b, k]).start()
    pltpu.make_async_copy(slr.at[k], lrb.at[b, k], lrr.at[b, k]).start()
    for dy, dk in ((0, 1), (1, 0), (1, 1)):
        d = (k + dk) % 2
        target = place(z, a, d, x, (b + dy) % 2)
        remote(slr.at[d], lrb.at[b, k], lrs.at[dy, dk], lrr.at[b, k], target).start()
        remote(sqg.at[d], qgb.at[b, k], qgs.at[dy, dk], qgr.at[b, k], target).start()

    for half in range(2):
        for part in range(2):
            done(bb.at[z, half, part], b1r.at[half, part])
    for dz in (1, 3, 2):
        remote(bb.at[z], bb.at[z], b2s.at[dz], b2r.at[z], at(dz=dz)).start()

    for half in range(2):
        for src in range(2):
            done(lrb.at[half, src], lrr.at[half, src])
            done(qgb.at[half, src], qgr.at[half, src])
        pack_queries(half, qgb, lrb, qp, gp)

    def block(t, carry):
        dx = (t + t // 2 - 2 * (t // 3)) % 4
        xk = (x + dx) % 4
        for src in range(2):
            done(kvb.at[xk, src], kvr.at[xk, src])
        pl.when(xk != z)(lambda: done(bb.at[xk], b2r.at[xk]))
        compute_block(kvb.at[xk], qp, gp, bb.at[xk], dkv.at[xk], dqb, dbb.at[xk], scr, t == 0)
        pl.when(xk != z)(
            remote(dbb.at[xk], rb.at[z], dbs.at[xk], dbr.at[z], place(xk, a, k, x, b)).start
        )
        for dk in (0, 1):
            d = (k + dk) % 2
            copy = remote(
                dkv.at[xk, d], rkv.at[x, k], dks.at[dx, dk], dkr.at[x, k], place(z, a, d, xk, b)
            )
            if dk == 0:
                pl.when(dx != 0)(copy.start)
            else:
                copy.start()
        return carry

    lax.fori_loop(0, 4, block, 0)

    for dy, dk in ((1, 0), (1, 1), (0, 1)):
        d = (k + dk) % 2
        to = (b + dy) % 2
        remote(
            dqb.at[to, d], rdq.at[b, k], dqs.at[dy, dk], dqr.at[b, k], place(z, a, d, x, to)
        ).start()

    for dz in (1, 3, 2):
        zk = (z + dz) % 4
        done(rb.at[zk], dbr.at[zk])
        for half in range(2):
            for part in range(2):
                for h in range(2):
                    dbb[z, half, part, h] += rb[zk, half, part, h]
    for dy in (0, 1):
        for dk in (0, 1):
            half = (b + dy) % 2
            part = (k + dk) % 2
            copy = remote(
                dbb.at[z, half, part], rbb.at[a, k], d1s.at[dy, dk], d1r.at[a, k],
                place(z, b, part, x, half),
            )
            if dy == 0 and dk == 0:
                pl.when(a == b)(
                    lambda: pltpu.make_async_copy(dbb.at[z, b, k], rbb.at[a, k], d1r.at[a, k]).start()
                )
                pl.when(a != b)(copy.start)
            else:
                copy.start()

    for dx in range(4):
        for dk in range(2):
            if dx or dk:
                done(rkv.at[(x + dx) % 4, (k + dk) % 2], dkr.at[(x + dx) % 4, (k + dk) % 2])
    for j in range(5):
        for which, out in ((0, dk_ref), (1, dv_ref)):
            own = dkv[x, k, which, j]
            for dx in (1, 2, 3):
                own = own + rkv[(x + dx) % 4, k, which, j]
            other = rkv[0, 1 - k, which, j]
            for xk in (1, 2, 3):
                other = other + rkv[xk, 1 - k, which, j]
            low = jnp.where(k == 0, own, other)
            high = jnp.where(k == 0, other, own)
            out[:, j, :] = jnp.concatenate([low, high], axis=0).T
    for dy, dk in ((1, 0), (1, 1), (0, 1)):
        done(rdq.at[(b + dy) % 2, (k + dk) % 2], dqr.at[(b + dy) % 2, (k + dk) % 2])
    for j in range(5):
        own = dqb[b, k, j] + rdq[1 - b, k, j]
        other = rdq[0, 1 - k, j] + rdq[1, 1 - k, j]
        low = jnp.where(k == 0, own, other)
        high = jnp.where(k == 0, other, own)
        dq_ref[:, j, :] = jnp.concatenate([low, high], axis=0).T
    for half in range(2):
        for part in range(2):
            done(rbb.at[half, part], d1r.at[half, part])
    for d in range(2):
        for h in range(2):
            db_ref[2 * d + h] = rbb[0, d, h] + rbb[1, d, h]

    for dx in range(4):
        for dk in range(2):
            if dx or dk:
                done(skv.at[0], kvs.at[dx, dk])
                done(dkv.at[0, 0], dks.at[dx, dk])
    for dy, dk in ((1, 0), (1, 1), (0, 1)):
        done(slr.at[0], lrs.at[dy, dk])
        done(sqg.at[0], qgs.at[dy, dk])
        done(dqb.at[0, 0], dqs.at[dy, dk])
    for da in (0, 1):
        for dk in (0, 1):
            if da or dk:
                done(sbb.at[0], b1s.at[da, dk])
                done(sbb.at[0], d1s.at[da, dk])

    def left():
        done(sbb.at[0], b1s.at[0, 0])
        done(sbb.at[0], d1s.at[0, 0])

    pl.when(a != b)(left)
    for dz in (1, 2, 3):
        done(bb.at[0], b2s.at[dz])
        done(dbb.at[0], dbs.at[(z + dz) % 4])


def body(query_proj, key_proj, value_proj, out_grad, pair_bias, log_sum_exp, correction, pad_mask):
    vmem = pl.BlockSpec(memory_space=pltpu.VMEM)
    f = lambda *shape: pltpu.VMEM(shape, F32)
    dma = lambda *shape: pltpu.SemaphoreType.DMA(shape)
    pair = [dma(2, 2)] * 2
    return pl.pallas_call(
        kernel,
        out_shape=[jax.ShapeDtypeStruct((256, 5, 128), F32)] * 3
        + [jax.ShapeDtypeStruct((4, 128, 256), F32)],
        in_specs=[vmem] * 8,
        out_specs=[vmem] * 4,
        scratch_shapes=[
            f(2, 2, 5, 64, 256),
            f(2, 2, 5, 64, 256),
            f(2, 2, 128, 256),
            f(2, 2, 2, 5, 256),
            f(4, 2, 2, 5, 64, 256),
            f(2, 2, 2, 5, 64, 256),
            f(2, 2, 2, 2, 5, 256),
            f(4, 2, 2, 2, 128, 256),
            f(4, 2, 2, 5, 64, 256),
            f(4, 2, 2, 5, 64, 256),
            f(2, 2, 5, 64, 256),
            f(2, 2, 5, 64, 256),
            f(4, 2, 2, 2, 128, 256),
            f(4, 2, 2, 2, 128, 256),
            f(2, 2, 2, 128, 256),
            pltpu.VMEM((2, 5, 2, 128, 512), BF),
            pltpu.VMEM((2, 5, 2, 128, 512), BF),
            pltpu.VMEM((2, 4, 256, 512), BF),
            dma(4, 2), dma(4, 2), *pair, *pair, *pair, dma(4), dma(4),
            dma(4, 2), dma(4, 2), *pair, dma(4), dma(4), *pair,
        ],
        compiler_params=pltpu.CompilerParams(
            collective_id=0, has_side_effects=True, vmem_limit_bytes=60 * 2**20
        ),
    )(
        query_proj, key_proj, value_proj, out_grad, pair_bias, log_sum_exp, correction,
        pad_mask.reshape(16, 128),
    )


def solution(mesh):
    return jax.shard_map(
        body,
        mesh=mesh,
        in_specs=(
            P("col", "row", None),
            P("col", "row", None),
            P("col", "row", None),
            P("col", "row", None),
            P(None, "row", "col"),
            P(None, "row", "col"),
            P(None, "row", "col"),
            P(),
        ),
        out_specs=(
            P("col", "row", None),
            P("col", "row", None),
            P("col", "row", None),
            P(None, "row", "col"),
        ),
        check_vma=False,
    )
```

```python
import functools
import math

import jax
import jax.numpy as jnp
from jax import lax
from jax.experimental import pallas as pl
from jax.experimental.pallas import tpu as pltpu
from jax.sharding import PartitionSpec as P

LOG2E = math.log2(math.e)
ROOT = 1.0 / math.sqrt(32)
BF = jnp.bfloat16
F32 = jnp.float32
MESH = pl.DeviceIdType.MESH


def place(z, a, k, x, b):
    return (z * 4 + a * 2 + k, x * 2 + b)


def dg(lhs, rhs, lhs_dim, rhs_dim):
    return lax.dot_general(
        lhs, rhs, (((lhs_dim,), (rhs_dim,)), ((), ())), preferred_element_type=F32
    )


def split(x):
    hi = x.astype(BF)
    return hi, (x - hi.astype(F32)).astype(BF)


def extra_rows(x):
    hi = x.astype(BF)
    rest = x - hi.astype(F32)
    mid = rest.astype(BF)
    low = (rest - mid.astype(F32)).astype(BF)
    row = lax.broadcasted_iota(jnp.int32, (32, x.shape[1]), 0)
    out = jnp.where(
        row == 0,
        hi.astype(F32),
        jnp.where(row == 1, mid.astype(F32), jnp.where(row == 2, low.astype(F32), 0.0)),
    )
    return out.astype(BF)


def key_rows(x):
    hi, low = split(x)
    ones = jnp.ones((32, x.shape[1]), BF)
    return hi, low, jnp.concatenate([hi, low, hi, ones], axis=0)


def pack_queries(h, qgb, lrb, qp, gp):
    def step(j, carry):
        for src in range(2):
            for half in range(2):
                cols = slice(256 * half, 256 * half + 256)
                level = lrb[half, src, 0, h, pl.ds(j, 1), :] * (-LOG2E)
                corr = -lrb[half, src, 1, h, pl.ds(j, 1), :]
                for which, packed, scale, row in (
                    (0, qp, LOG2E * ROOT, level),
                    (1, gp, None, corr),
                ):
                    x = qgb[h, half, src, which, j]
                    hi, low = split(x if scale is None else x * scale)
                    packed[h, src, j, 0:32, cols] = hi
                    packed[h, src, j, 32:64, cols] = hi
                    packed[h, src, j, 64:96, cols] = low
                    packed[h, src, j, 96:128, cols] = extra_rows(row)
        return carry

    lax.fori_loop(0, 5, step, 0)


def compute_block(kv, qp, gp, bias, dkv, dqb, db, scr, first):
    for half in range(2):
        for part in range(2):
            db[half, part] = jnp.zeros((128, 256), F32)

    def step(j, carry):
        for src in range(2):
            w_hi, w_low, s_hi, s_low = [scr.at[src, i] for i in range(4)]
            k_hi, k_low, kp = key_rows(kv[src, 0, j])
            _, _, vp = key_rows(kv[src, 1, j])
            for half in range(2):
                cols = slice(256 * half, 256 * half + 256)
                st = dg(kp, qp[src, j, :, cols], 0, 0)
                pt = dg(vp, gp[src, j, :, cols], 0, 0)
                for part in range(2):
                    keys = slice(128 * part, 128 * part + 128)
                    w = jnp.exp2(st[keys] + bias[half, part])
                    ds = w * pt[keys]
                    db[half, part] += ds
                    w_hi[keys, cols], w_low[keys, cols] = split(w)
                    s_hi[keys, cols], s_low[keys, cols] = split(ds)
            k2 = jnp.concatenate([k_hi, k_low], axis=0)
            r = dg(k2, s_hi[...], 1, 0)
            total = (r[:32] + r[32:] + dg(k_hi, s_low[...], 1, 0)) * ROOT
            for half in range(2):
                mine = total[:, 256 * half : 256 * half + 256]
                dqb[half, src, j] = jnp.where(first, mine, dqb[half, src, j] + mine)
            r = dg(qp[src, j, 32:96, :], s_hi[...], 1, 1)
            r2 = dg(qp[src, j, 0:32, :], s_low[...], 1, 1)
            dkv[src, 0, j] = (r[:32] + r[32:] + r2) * (1.0 / LOG2E)
            r = dg(gp[src, j, 32:96, :], w_hi[...], 1, 1)
            r2 = dg(gp[src, j, 0:32, :], w_low[...], 1, 1)
            dkv[src, 1, j] = r[:32] + r[32:] + r2
        return carry

    lax.fori_loop(0, 5, step, 0)


def kernel(
    q_ref, k_ref, v_ref, g_ref, b_ref, l_ref, r_ref, m_ref,
    dq_ref, dk_ref, dv_ref, db_ref,
    skv, sqg, sbb, slr, kvb, qgb, lrb, bb, dkv, rkv, dqb, rdq, dbb, rb, rbb, qp, gp, scr,
    kvs, kvr, qgs, qgr, lrs, lrr, b1s, b1r, b2s, b2r, dks, dkr, dqs, dqr, dbs, dbr, d1s, d1r,
):
    row = lax.axis_index("row")
    col = lax.axis_index("col")
    z = row // 4
    a = (row // 2) % 2
    k = row % 2
    x = col // 2
    b = col % 2
    right, left = (x + 1) % 4, (x + 3) % 4
    up, down = (z + 1) % 4, (z + 3) % 4

    def at(dz=0, dx=0, dk=0):
        return place((z + dz) % 4, a, (k + dk) % 2, (x + dx) % 4, b)

    barrier = pltpu.get_barrier_semaphore()
    partners = [at(dx=dx, dk=dk) for dx in (1, 2, 3) for dk in (0, 1)]
    partners += [at(dz=dz) for dz in (1, 2, 3)]
    for da in (0, 1):
        for dy in (0, 1):
            for dk in (0, 1):
                if da or dy or dk:
                    partners.append(place(z, (a + da) % 2, (k + dk) % 2, x, (b + dy) % 2))
    for partner in partners:
        pl.semaphore_signal(barrier, inc=1, device_id=partner, device_id_type=MESH)

    def remote(src, dst, send, recv, target):
        return pltpu.make_async_remote_copy(
            src_ref=src, dst_ref=dst, send_sem=send, recv_sem=recv,
            device_id=target, device_id_type=MESH,
        )

    def done(ref, sem):
        pltpu.make_async_copy(ref, ref, sem).wait()

    def turn(ref, dst, which):
        for j in range(5):
            t = ref[j].T
            for d in range(2):
                for h in range(2):
                    first = 64 * d + 32 * h
                    dst[h, d, which, j] = t[first : first + 32]

    def send_bias(h):
        for da in (0, 1):
            for dk in (0, 1):
                a_to = (a + da) % 2
                d = (k + dk) % 2
                copy = remote(
                    sbb.at[h, d], bb.at[h, z, b, k], b1s.at[h, da, dk], b1r.at[h, b, k],
                    place(z, a_to, d, x, a),
                )
                if da == 0 and dk == 0:
                    own = pltpu.make_async_copy(sbb.at[h, k], bb.at[h, z, b, k], b1r.at[h, b, k])
                    pl.when(a == b)(own.start)
                    pl.when(a != b)(copy.start)
                else:
                    copy.start()

    def spread_bias(h):
        for half in range(2):
            for part in range(2):
                done(bb.at[h, z, half, part], b1r.at[h, half, part])
        for i, (to, half) in enumerate(((1, 0), (3, 1), (1, 1), (3, 0))):
            remote(
                bb.at[h, z, half], bb.at[h, z, half], b2s.at[h, i], b2r.at[h, z, half], at(dz=to)
            ).start()

    def pass_bias(h):
        done(bb.at[h, down, 0], b2r.at[h, down, 0])
        remote(
            bb.at[h, down, 0], bb.at[h, down, 0], b2s.at[h, 4], b2r.at[h, down, 0], at(dz=1)
        ).start()
        done(bb.at[h, up, 1], b2r.at[h, up, 1])
        remote(
            bb.at[h, up, 1], bb.at[h, up, 1], b2s.at[h, 5], b2r.at[h, up, 1], at(dz=3)
        ).start()

    def wait_bias(h, zk):
        def rest(half):
            passed = (half == 0) & (zk == down) | (half == 1) & (zk == up)
            pl.when((zk != z) & jnp.logical_not(passed))(
                lambda: done(bb.at[h, zk, half], b2r.at[h, zk, half])
            )

        rest(0)
        rest(1)

    def send_keys(h):
        pltpu.make_async_copy(skv.at[h, k], kvb.at[h, x, k], kvr.at[h, x, k]).start()
        for i, (dx, dk) in enumerate(((1, 0), (3, 0), (1, 1), (3, 1), (0, 1))):
            remote(
                skv.at[h, (k + dk) % 2], kvb.at[h, x, k], kvs.at[h, i], kvr.at[h, x, k],
                at(dx=dx, dk=dk),
            ).start()

    def pass_keys(h):
        done(kvb.at[h, left, 0], kvr.at[h, left, 0])
        remote(
            kvb.at[h, left, 0], kvb.at[h, left, 0], kvs.at[h, 5], kvr.at[h, left, 0], at(dx=1)
        ).start()
        done(kvb.at[h, right, 1], kvr.at[h, right, 1])
        remote(
            kvb.at[h, right, 1], kvb.at[h, right, 1], kvs.at[h, 6], kvr.at[h, right, 1], at(dx=3)
        ).start()

    def wait_keys(h, xk):
        pl.when(xk != left)(lambda: done(kvb.at[h, xk, 0], kvr.at[h, xk, 0]))
        pl.when(xk != right)(lambda: done(kvb.at[h, xk, 1], kvr.at[h, xk, 1]))

    def send_queries(h):
        pltpu.make_async_copy(sqg.at[h, k], qgb.at[h, b, k], qgr.at[h, b, k]).start()
        for dy, dk in ((1, 0), (1, 1), (0, 1)):
            d = (k + dk) % 2
            remote(
                sqg.at[h, d], qgb.at[h, b, k], qgs.at[h, dy, dk], qgr.at[h, b, k],
                place(z, a, d, x, (b + dy) % 2),
            ).start()

    def wait_queries(h):
        for half in range(2):
            for src in range(2):
                done(qgb.at[h, half, src], qgr.at[h, half, src])

    def sum_bias(h):
        for dz in (1, 3, 2):
            zk = (z + dz) % 4
            done(rb.at[h, zk], dbr.at[h, zk])
        for half in range(2):
            for part in range(2):
                dbb[h, z, half, part] += (
                    rb[h, up, half, part] + rb[h, down, half, part]
                ) + rb[h, (z + 2) % 4, half, part]
        for dy in (1, 0):
            for dk in (0, 1):
                half = (b + dy) % 2
                part = (k + dk) % 2
                copy = remote(
                    dbb.at[h, z, half, part], rbb.at[h, a, k], d1s.at[h, dy, dk], d1r.at[h, a, k],
                    place(z, b, part, x, half),
                )
                if dy == 0 and dk == 0:
                    own = pltpu.make_async_copy(dbb.at[h, z, b, k], rbb.at[h, a, k], d1r.at[h, a, k])
                    pl.when(a == b)(own.start)
                    pl.when(a != b)(copy.start)
                else:
                    copy.start()

    def send_query_grads(h):
        for dy, dk in ((1, 0), (1, 1), (0, 1)):
            d = (k + dk) % 2
            to = (b + dy) % 2
            remote(
                dqb.at[h, to, d], rdq.at[h, b, k], dqs.at[h, dy, dk], dqr.at[h, b, k],
                place(z, a, d, x, to),
            ).start()

    alive = jnp.broadcast_to(m_ref[pl.ds(row, 1), :], (128, 128)).astype(F32).T
    alive = jnp.concatenate([alive, alive], axis=1) == 1.0
    for h in range(4):
        sbb[h % 2, h // 2] = jnp.where(alive, b_ref[h] * LOG2E, -1e30)
    for d in range(2):
        for h in range(2):
            slr[d, 0, h] = l_ref[:, 2 * d + h, :]
            slr[d, 1, h] = r_ref[:, 2 * d + h, :]

    pl.semaphore_wait(barrier, len(partners))

    send_bias(0)
    turn(k_ref, skv, 0)
    turn(v_ref, skv, 1)
    send_keys(0)
    pltpu.make_async_copy(slr.at[k], lrb.at[b, k], lrr.at[b, k]).start()
    for dy, dk in ((1, 0), (1, 1), (0, 1)):
        d = (k + dk) % 2
        remote(
            slr.at[d], lrb.at[b, k], lrs.at[dy, dk], lrr.at[b, k], place(z, a, d, x, (b + dy) % 2)
        ).start()
    turn(q_ref, sqg, 0)
    turn(g_ref, sqg, 1)
    send_queries(0)
    spread_bias(0)
    pass_keys(0)
    send_keys(1)
    for half in range(2):
        for src in range(2):
            done(lrb.at[half, src], lrr.at[half, src])
    wait_queries(0)
    send_bias(1)
    send_queries(1)
    pack_queries(0, qgb, lrb, qp, gp)
    pass_bias(0)

    def block(n, carry):
        h = n // 4
        t = n % 4
        xk = (x + z + 1 + t) % 4

        @pl.when(n == 4)
        def _():
            wait_queries(1)
            pack_queries(1, qgb, lrb, qp, gp)

        wait_keys(h, xk)
        wait_bias(h, xk)
        compute_block(
            kvb.at[h, xk], qp.at[h], gp.at[h], bb.at[h, xk], dkv.at[h, xk], dqb.at[h],
            dbb.at[h, xk], scr, t == 0,
        )
        pl.when(xk != z)(
            remote(
                dbb.at[h, xk], rb.at[h, z], dbs.at[h, xk], dbr.at[h, z], place(xk, a, k, x, b)
            ).start
        )
        for dk in (0, 1):
            d = (k + dk) % 2
            copy = remote(
                dkv.at[h, xk, d], rkv.at[h, x, k], dks.at[h, xk, dk], dkr.at[h, x, k],
                place(z, a, d, xk, b),
            )
            if dk == 0:
                pl.when(xk != x)(copy.start)
            else:
                copy.start()

        @pl.when(n == 0)
        def _():
            spread_bias(1)

        @pl.when(n == 1)
        def _():
            pass_keys(1)

        @pl.when(n == 2)
        def _():
            pass_bias(1)

        @pl.when(n == 3)
        def _():
            send_query_grads(0)

        @pl.when(n == 5)
        def _():
            sum_bias(0)

        return carry

    lax.fori_loop(0, 8, block, 0)
    send_query_grads(1)
    sum_bias(1)

    for h in range(2):
        for dx in range(4):
            for dk in range(2):
                if dx or dk:
                    xk = (x + dx) % 4
                    c = (k + dk) % 2
                    done(rkv.at[h, xk, c], dkr.at[h, xk, c])

    def join(own, other):
        low = jnp.where(k == 0, own, other)
        high = jnp.where(k == 0, other, own)
        return jnp.concatenate([low, high], axis=0).T

    def rows(ref, *index):
        return jnp.concatenate([ref[(0, *index)], ref[(1, *index)]], axis=0)

    for j in range(5):
        for which, out in ((0, dk_ref), (1, dv_ref)):
            own = rows(dkv, x, k, which, j)
            for dx in (1, 2, 3):
                own = own + rows(rkv, (x + dx) % 4, k, which, j)
            other = rows(rkv, 0, 1 - k, which, j)
            for xk in (1, 2, 3):
                other = other + rows(rkv, xk, 1 - k, which, j)
            out[j] = join(own, other)
    for h in range(2):
        for dy, dk in ((1, 0), (1, 1), (0, 1)):
            done(rdq.at[h, (b + dy) % 2, (k + dk) % 2], dqr.at[h, (b + dy) % 2, (k + dk) % 2])
    for j in range(5):
        own = rows(dqb, b, k, j) + rows(rdq, 1 - b, k, j)
        other = rows(rdq, 0, 1 - k, j) + rows(rdq, 1, 1 - k, j)
        dq_ref[j] = join(own, other)
    for h in range(2):
        for half in range(2):
            for part in range(2):
                done(rbb.at[h, half, part], d1r.at[h, half, part])
        for d in range(2):
            db_ref[2 * d + h] = rbb[h, 0, d] + rbb[h, 1, d]

    for h in range(2):
        for i in range(7):
            done(skv.at[0, 0], kvs.at[h, i])
        for dx in range(4):
            done(dkv.at[0, 0, 0], dks.at[h, (x + dx) % 4, 1])
            if dx:
                done(dkv.at[0, 0, 0], dks.at[h, (x + dx) % 4, 0])
        for dy, dk in ((1, 0), (1, 1), (0, 1)):
            done(sqg.at[0, 0], qgs.at[h, dy, dk])
            done(dqb.at[0, 0, 0], dqs.at[h, dy, dk])
            done(sbb.at[0, 0], b1s.at[h, dy, dk])
            done(sbb.at[0, 0], d1s.at[h, dy, dk])
        for i in range(6):
            done(bb.at[0, 0, 0], b2s.at[h, i])
        for dz in (1, 2, 3):
            done(dbb.at[0, 0], dbs.at[h, (z + dz) % 4])
    for dy, dk in ((1, 0), (1, 1), (0, 1)):
        done(slr.at[0], lrs.at[dy, dk])

    @pl.when(a != b)
    def _():
        for h in range(2):
            done(sbb.at[0, 0], b1s.at[h, 0, 0])
            done(sbb.at[0, 0], d1s.at[h, 0, 0])


def body(query_proj, key_proj, value_proj, out_grad, pair_bias, log_sum_exp, correction, pad_mask):
    vmem = pl.BlockSpec(memory_space=pltpu.VMEM)
    f = lambda *shape: pltpu.VMEM(shape, F32)
    dma = lambda *shape: pltpu.SemaphoreType.DMA(shape)
    swap = lambda y: jnp.transpose(y, (1, 0, 2))
    pair = [dma(2, 2, 2)] * 2
    dq, dk, dv, db = pl.pallas_call(
        kernel,
        out_shape=[jax.ShapeDtypeStruct((5, 256, 128), F32)] * 3
        + [jax.ShapeDtypeStruct((4, 128, 256), F32)],
        in_specs=[vmem] * 8,
        out_specs=[vmem] * 4,
        scratch_shapes=[
            f(2, 2, 2, 5, 32, 256),
            f(2, 2, 2, 5, 32, 256),
            f(2, 2, 128, 256),
            f(2, 2, 2, 5, 256),
            f(2, 4, 2, 2, 5, 32, 256),
            f(2, 2, 2, 2, 5, 32, 256),
            f(2, 2, 2, 2, 5, 256),
            f(2, 4, 2, 2, 128, 256),
            f(2, 4, 2, 2, 5, 32, 256),
            f(2, 4, 2, 2, 5, 32, 256),
            f(2, 2, 2, 5, 32, 256),
            f(2, 2, 2, 5, 32, 256),
            f(2, 4, 2, 2, 128, 256),
            f(2, 4, 2, 2, 128, 256),
            f(2, 2, 2, 128, 256),
            pltpu.VMEM((2, 2, 5, 128, 512), BF),
            pltpu.VMEM((2, 2, 5, 128, 512), BF),
            pltpu.VMEM((2, 4, 256, 512), BF),
            dma(2, 7), dma(2, 4, 2), *pair, dma(2, 2), dma(2, 2), *pair, dma(2, 6), dma(2, 4, 2),
            dma(2, 4, 2), dma(2, 4, 2), *pair, dma(2, 4), dma(2, 4), *pair,
        ],
        compiler_params=pltpu.CompilerParams(
            collective_id=0, has_side_effects=True, vmem_limit_bytes=60 * 2**20
        ),
    )(
        swap(query_proj), swap(key_proj), swap(value_proj), swap(out_grad), pair_bias,
        swap(log_sum_exp), swap(correction), pad_mask.reshape(16, 128),
    )
    return swap(dq), swap(dk), swap(dv), db


def solution(mesh):
    return jax.shard_map(
        body,
        mesh=mesh,
        in_specs=(
            P("col", "row", None),
            P("col", "row", None),
            P("col", "row", None),
            P("col", "row", None),
            P(None, "row", "col"),
            P(None, "row", "col"),
            P(None, "row", "col"),
            P(),
        ),
        out_specs=(
            P("col", "row", None),
            P("col", "row", None),
            P("col", "row", None),
            P(None, "row", "col"),
        ),
        check_vma=False,
    )
```

```python
import functools
import math

import jax
import jax.numpy as jnp
from jax import lax
from jax.experimental import pallas as pl
from jax.experimental.pallas import tpu as pltpu
from jax.sharding import PartitionSpec as P

LOG2E = math.log2(math.e)
ROOT = 1.0 / math.sqrt(32)
BF = jnp.bfloat16
F32 = jnp.float32
MESH = pl.DeviceIdType.MESH


def place(z, a, k, x, b):
    return (z * 4 + a * 2 + k, x * 2 + b)


def dg(lhs, rhs, lhs_dim, rhs_dim):
    return lax.dot_general(
        lhs, rhs, (((lhs_dim,), (rhs_dim,)), ((), ())), preferred_element_type=F32
    )


def split(x):
    hi = x.astype(BF)
    return hi, (x - hi.astype(F32)).astype(BF)


def extra_rows(x):
    hi = x.astype(BF)
    rest = x - hi.astype(F32)
    mid = rest.astype(BF)
    low = (rest - mid.astype(F32)).astype(BF)
    row = lax.broadcasted_iota(jnp.int32, (32, x.shape[1]), 0)
    out = jnp.where(
        row == 0,
        hi.astype(F32),
        jnp.where(row == 1, mid.astype(F32), jnp.where(row == 2, low.astype(F32), 0.0)),
    )
    return out.astype(BF)


def key_rows(x):
    hi, low = split(x)
    ones = jnp.ones((32, x.shape[1]), BF)
    return hi, low, jnp.concatenate([hi, low, hi, ones], axis=0)


def pack_queries(h, qgb, lrb, qp, gp):
    def step(j, carry):
        for src in range(2):
            for half in range(2):
                cols = slice(256 * half, 256 * half + 256)
                level = lrb[half, src, 0, h, pl.ds(j, 1), :] * (-LOG2E)
                corr = -lrb[half, src, 1, h, pl.ds(j, 1), :]
                for which, packed, scale, row in (
                    (0, qp, LOG2E * ROOT, level),
                    (1, gp, None, corr),
                ):
                    x = qgb[h, half, src, which, j]
                    hi, low = split(x if scale is None else x * scale)
                    packed[h, src, j, 0:32, cols] = hi
                    packed[h, src, j, 32:64, cols] = hi
                    packed[h, src, j, 64:96, cols] = low
                    packed[h, src, j, 96:128, cols] = extra_rows(row)
        return carry

    lax.fori_loop(0, 5, step, 0)


def compute_block(kv, qp, gp, bias, dkv, dqb, db, scr, first):
    for half in range(2):
        for part in range(2):
            db[half, part] = jnp.zeros((128, 256), F32)

    def step(j, carry):
        keys = [None, None]
        scores = [None, None]
        grads = [None, None]
        for src in range(2):
            k_hi, k_low, kp = key_rows(kv[src, 0, j])
            _, _, vp = key_rows(kv[src, 1, j])
            keys[src] = (k_hi, k_low)
            scores[src] = dg(kp, qp[src, j], 0, 0)
            grads[src] = dg(vp, gp[src, j], 0, 0)
        for src in range(2):
            w_hi, w_low, s_hi, s_low = [scr.at[src, i] for i in range(4)]
            for half in range(2):
                cols = slice(256 * half, 256 * half + 256)
                for part in range(2):
                    rows = slice(128 * part, 128 * part + 128)
                    w = jnp.exp2(scores[src][rows, cols] + bias[half, part])
                    ds = w * grads[src][rows, cols]
                    db[half, part] += ds
                    w_hi[rows, cols], w_low[rows, cols] = split(w)
                    s_hi[rows, cols], s_low[rows, cols] = split(ds)
        for src in range(2):
            w_hi, w_low, s_hi, s_low = [scr.at[src, i] for i in range(4)]
            k_hi, k_low = keys[src]
            r = dg(jnp.concatenate([k_hi, k_low], axis=0), s_hi[...], 1, 0)
            total = (r[:32] + r[32:] + dg(k_hi, s_low[...], 1, 0)) * ROOT
            for half in range(2):
                mine = total[:, 256 * half : 256 * half + 256]
                dqb[half, src, j] = jnp.where(first, mine, dqb[half, src, j] + mine)
            r = dg(qp[src, j, 32:96, :], s_hi[...], 1, 1)
            r2 = dg(qp[src, j, 0:32, :], s_low[...], 1, 1)
            dkv[src, 0, j] = (r[:32] + r[32:] + r2) * (1.0 / LOG2E)
            r = dg(gp[src, j, 32:96, :], w_hi[...], 1, 1)
            r2 = dg(gp[src, j, 0:32, :], w_low[...], 1, 1)
            dkv[src, 1, j] = r[:32] + r[32:] + r2
        return carry

    lax.fori_loop(0, 5, step, 0)


def kernel(
    q_ref, k_ref, v_ref, g_ref, b_ref, l_ref, r_ref, m_ref,
    dq_ref, dk_ref, dv_ref, db_ref,
    skv, sqg, sbb, slr, kvb, qgb, lrb, bb, dkv, rkv, rel, zrel, dqb, rdq, dbb, rb, rbb, qp, gp, scr,
    kvs, kvr, qgs, qgr, lrs, lrr, b1s, b1r, b2s, b2r, dks, dkr, rls, rlr, dqs, dqr, zls, zlr, dbs, dbr, d1s, d1r,
):
    row = lax.axis_index("row")
    col = lax.axis_index("col")
    z = row // 4
    a = (row // 2) % 2
    k = row % 2
    x = col // 2
    b = col % 2
    right, left = (x + 1) % 4, (x + 3) % 4
    up, down = (z + 1) % 4, (z + 3) % 4

    def at(dz=0, dx=0, dk=0):
        return place((z + dz) % 4, a, (k + dk) % 2, (x + dx) % 4, b)

    barrier = pltpu.get_barrier_semaphore()
    partners = [at(dx=dx, dk=dk) for dx in (1, 3) for dk in (0, 1)]
    partners += [at(dz=dz) for dz in (1, 3)]
    for da in (0, 1):
        for dy in (0, 1):
            for dk in (0, 1):
                if da or dy or dk:
                    partners.append(place(z, (a + da) % 2, (k + dk) % 2, x, (b + dy) % 2))
    for partner in partners:
        pl.semaphore_signal(barrier, inc=1, device_id=partner, device_id_type=MESH)

    def remote(src, dst, send, recv, target):
        return pltpu.make_async_remote_copy(
            src_ref=src, dst_ref=dst, send_sem=send, recv_sem=recv,
            device_id=target, device_id_type=MESH,
        )

    def done(ref, sem):
        pltpu.make_async_copy(ref, ref, sem).wait()

    def turn(ref, dst, which):
        for j in range(5):
            t = ref[j].T
            for d in range(2):
                for h in range(2):
                    first = 64 * d + 32 * h
                    dst[h, d, which, j] = t[first : first + 32]

    def send_bias(h):
        for da in (0, 1):
            for dk in (0, 1):
                a_to = (a + da) % 2
                d = (k + dk) % 2
                copy = remote(
                    sbb.at[h, d], bb.at[h, z, b, k], b1s.at[h, da, dk], b1r.at[h, b, k],
                    place(z, a_to, d, x, a),
                )
                if da == 0 and dk == 0:
                    own = pltpu.make_async_copy(sbb.at[h, k], bb.at[h, z, b, k], b1r.at[h, b, k])
                    pl.when(a == b)(own.start)
                    pl.when(a != b)(copy.start)
                else:
                    copy.start()

    def spread_bias(h):
        for half in range(2):
            for part in range(2):
                done(bb.at[h, z, half, part], b1r.at[h, half, part])
        for i, (to, half) in enumerate(((1, 0), (3, 1), (1, 1), (3, 0))):
            remote(
                bb.at[h, z, half], bb.at[h, z, half], b2s.at[h, i], b2r.at[h, z, half], at(dz=to)
            ).start()

    def pass_bias(h):
        done(bb.at[h, down, 0], b2r.at[h, down, 0])
        remote(
            bb.at[h, down, 0], bb.at[h, down, 0], b2s.at[h, 4], b2r.at[h, down, 0], at(dz=1)
        ).start()
        done(bb.at[h, up, 1], b2r.at[h, up, 1])
        remote(
            bb.at[h, up, 1], bb.at[h, up, 1], b2s.at[h, 5], b2r.at[h, up, 1], at(dz=3)
        ).start()

    def wait_bias(h, zk):
        def rest(half):
            passed = (half == 0) & (zk == down) | (half == 1) & (zk == up)
            pl.when((zk != z) & jnp.logical_not(passed))(
                lambda: done(bb.at[h, zk, half], b2r.at[h, zk, half])
            )

        rest(0)
        rest(1)

    def send_keys(h):
        pltpu.make_async_copy(skv.at[h, k], kvb.at[h, x, k], kvr.at[h, x, k]).start()
        for i, (dx, dk) in enumerate(((1, 0), (3, 0), (1, 1), (3, 1), (0, 1))):
            remote(
                skv.at[h, (k + dk) % 2], kvb.at[h, x, k], kvs.at[h, i], kvr.at[h, x, k],
                at(dx=dx, dk=dk),
            ).start()

    def pass_keys(h):
        done(kvb.at[h, left, 0], kvr.at[h, left, 0])
        remote(
            kvb.at[h, left, 0], kvb.at[h, left, 0], kvs.at[h, 5], kvr.at[h, left, 0], at(dx=1)
        ).start()
        done(kvb.at[h, right, 1], kvr.at[h, right, 1])
        remote(
            kvb.at[h, right, 1], kvb.at[h, right, 1], kvs.at[h, 6], kvr.at[h, right, 1], at(dx=3)
        ).start()

    def wait_keys(h, xk):
        pl.when(xk != left)(lambda: done(kvb.at[h, xk, 0], kvr.at[h, xk, 0]))
        pl.when(xk != right)(lambda: done(kvb.at[h, xk, 1], kvr.at[h, xk, 1]))

    def send_queries(h):
        pltpu.make_async_copy(sqg.at[h, k], qgb.at[h, b, k], qgr.at[h, b, k]).start()
        for dy, dk in ((1, 0), (1, 1), (0, 1)):
            d = (k + dk) % 2
            remote(
                sqg.at[h, d], qgb.at[h, b, k], qgs.at[h, dy, dk], qgr.at[h, b, k],
                place(z, a, d, x, (b + dy) % 2),
            ).start()

    def wait_queries(h):
        for half in range(2):
            for src in range(2):
                done(qgb.at[h, half, src], qgr.at[h, half, src])

    def push_bias_grad(h, to, half):
        zk = (up, down)[to]
        remote(
            dbb.at[h, zk, half], rb.at[h, to, half], dbs.at[h, to, half], dbr.at[h, to, half],
            place(zk, a, k, x, b),
        ).start()

    def send_bias_grad(h, zk):
        @pl.when(zk == (z + 2) % 4)
        def _():
            for half, dz in ((0, 1), (1, 3)):
                remote(
                    dbb.at[h, zk, half], zrel.at[h, half], zls.at[h, half], zlr.at[h, half],
                    at(dz=dz),
                ).start()

        pl.when(zk == up)(lambda: push_bias_grad(h, 0, 1))
        pl.when(zk == down)(lambda: push_bias_grad(h, 1, 0))

    def finish_bias_grad(h, zk):
        def finish(to):
            half = to
            done(zrel.at[h, half], zlr.at[h, half])
            for part in range(2):
                dbb[h, zk, half, part] += zrel[h, half, part]
            push_bias_grad(h, to, half)

        pl.when(zk == up)(lambda: finish(0))
        pl.when(zk == down)(lambda: finish(1))

    def sum_bias(h):
        for to in range(2):
            for half in range(2):
                done(rb.at[h, to, half], dbr.at[h, to, half])
        for half in range(2):
            for part in range(2):
                dbb[h, z, half, part] += rb[h, 0, half, part] + rb[h, 1, half, part]
        for dy in (1, 0):
            for dk in (0, 1):
                half = (b + dy) % 2
                part = (k + dk) % 2
                copy = remote(
                    dbb.at[h, z, half, part], rbb.at[h, a, k], d1s.at[h, dy, dk], d1r.at[h, a, k],
                    place(z, b, part, x, half),
                )
                if dy == 0 and dk == 0:
                    own = pltpu.make_async_copy(dbb.at[h, z, b, k], rbb.at[h, a, k], d1r.at[h, a, k])
                    pl.when(a == b)(own.start)
                    pl.when(a != b)(copy.start)
                else:
                    copy.start()

    def send_key_grads(h, xk, d):
        remote(
            dkv.at[h, xk, d], rkv.at[h, x, k], dks.at[h, xk, d], dkr.at[h, x, k],
            place(z, a, d, xk, b),
        ).start()

    def add_passed(h, xk, d):
        done(rel.at[h, d], rlr.at[h, d])
        for which in range(2):
            for j in range(5):
                dkv[h, xk, d, which, j] += rel[h, d, which, j]

    def send_query_grads(h):
        for dy, dk in ((1, 0), (1, 1), (0, 1)):
            d = (k + dk) % 2
            to = (b + dy) % 2
            remote(
                dqb.at[h, to, d], rdq.at[h, b, k], dqs.at[h, dy, dk], dqr.at[h, b, k],
                place(z, a, d, x, to),
            ).start()

    alive = jnp.broadcast_to(m_ref[pl.ds(row, 1), :], (128, 128)).astype(F32).T
    alive = jnp.concatenate([alive, alive], axis=1) == 1.0
    for h in range(4):
        sbb[h % 2, h // 2] = jnp.where(alive, b_ref[h] * LOG2E, -1e30)
    for d in range(2):
        for h in range(2):
            slr[d, 0, h] = l_ref[:, 2 * d + h, :]
            slr[d, 1, h] = r_ref[:, 2 * d + h, :]

    pl.semaphore_wait(barrier, len(partners))

    send_bias(0)
    turn(k_ref, skv, 0)
    turn(v_ref, skv, 1)
    send_keys(0)
    pltpu.make_async_copy(slr.at[k], lrb.at[b, k], lrr.at[b, k]).start()
    for dy, dk in ((1, 0), (1, 1), (0, 1)):
        d = (k + dk) % 2
        remote(
            slr.at[d], lrb.at[b, k], lrs.at[dy, dk], lrr.at[b, k], place(z, a, d, x, (b + dy) % 2)
        ).start()
    turn(q_ref, sqg, 0)
    turn(g_ref, sqg, 1)
    send_queries(0)
    spread_bias(0)
    pass_keys(0)
    send_keys(1)
    for half in range(2):
        for src in range(2):
            done(lrb.at[half, src], lrr.at[half, src])
    wait_queries(0)
    send_bias(1)
    pack_queries(0, qgb, lrb, qp, gp)
    pass_bias(0)

    def block_of(t):
        return (x + 2 + 3 * t + 3 * (t // 2) + 2 * (t // 3)) % 4

    def block(n, carry):
        h = n // 4
        t = n % 4
        xk = block_of(t)

        @pl.when(n == 4)
        def _():
            wait_queries(1)
            pack_queries(1, qgb, lrb, qp, gp)

        wait_keys(h, xk)
        wait_bias(h, xk)
        compute_block(
            kvb.at[h, xk], qp.at[h], gp.at[h], bb.at[h, xk], dkv.at[h, xk], dqb.at[h],
            dbb.at[h, xk], scr, t == 0,
        )
        send_bias_grad(h, xk)

        @pl.when(n > 0)
        def _():
            finish_bias_grad((n - 1) // 4, block_of((n - 1) % 4))


        @pl.when(t == 0)
        def _():
            for d, dx in ((0, 1), (1, 3)):
                remote(
                    dkv.at[h, xk, d], rel.at[h, d], rls.at[h, d], rlr.at[h, d], at(dx=dx)
                ).start()

        @pl.when(t == 1)
        def _():
            send_key_grads(h, right, 1)

        @pl.when(t == 2)
        def _():
            add_passed(h, right, 0)
            send_key_grads(h, right, 0)
            send_key_grads(h, left, 0)

        @pl.when(t == 3)
        def _():
            send_key_grads(h, x, 1 - k)
            add_passed(h, left, 1)
            send_key_grads(h, left, 1)

        @pl.when(n == 0)
        def _():
            spread_bias(1)
            send_queries(1)

        @pl.when(n == 1)
        def _():
            pass_keys(1)

        @pl.when(n == 2)
        def _():
            pass_bias(1)

        @pl.when(n == 3)
        def _():
            send_query_grads(0)

        @pl.when(n == 5)
        def _():
            sum_bias(0)

        return carry

    lax.fori_loop(0, 8, block, 0)
    finish_bias_grad(1, x)
    send_query_grads(1)

    for h in range(2):
        done(rkv.at[h, x, 1 - k], dkr.at[h, x, 1 - k])
        for xk in (right, left):
            for c in range(2):
                done(rkv.at[h, xk, c], dkr.at[h, xk, c])

    def join(own, other):
        low = jnp.where(k == 0, own, other)
        high = jnp.where(k == 0, other, own)
        return jnp.concatenate([low, high], axis=0).T

    def rows(ref, *index):
        return jnp.concatenate([ref[(0, *index)], ref[(1, *index)]], axis=0)

    for j in range(5):
        for which, out in ((0, dk_ref), (1, dv_ref)):
            own = rows(dkv, x, k, which, j)
            other = rows(rkv, x, 1 - k, which, j)
            for xk in (right, left):
                own = own + rows(rkv, xk, k, which, j)
                other = other + rows(rkv, xk, 1 - k, which, j)
            out[j] = join(own, other)
    sum_bias(1)
    for h in range(2):
        for dy, dk in ((1, 0), (1, 1), (0, 1)):
            done(rdq.at[h, (b + dy) % 2, (k + dk) % 2], dqr.at[h, (b + dy) % 2, (k + dk) % 2])
    for j in range(5):
        own = rows(dqb, b, k, j) + rows(rdq, 1 - b, k, j)
        other = rows(rdq, 0, 1 - k, j) + rows(rdq, 1, 1 - k, j)
        dq_ref[j] = join(own, other)
    for h in range(2):
        for half in range(2):
            for part in range(2):
                done(rbb.at[h, half, part], d1r.at[h, half, part])
        for d in range(2):
            db_ref[2 * d + h] = rbb[h, 0, d] + rbb[h, 1, d]

    for h in range(2):
        for i in range(7):
            done(skv.at[0, 0], kvs.at[h, i])
        done(dkv.at[0, 0, 0], dks.at[h, x, 1 - k])
        for d in range(2):
            done(dkv.at[0, 0, 0], dks.at[h, right, d])
            done(dkv.at[0, 0, 0], dks.at[h, left, d])
            done(rel.at[0, 0], rls.at[h, d])
        for dy, dk in ((1, 0), (1, 1), (0, 1)):
            done(sqg.at[0, 0], qgs.at[h, dy, dk])
            done(dqb.at[0, 0, 0], dqs.at[h, dy, dk])
            done(sbb.at[0, 0], b1s.at[h, dy, dk])
            done(sbb.at[0, 0], d1s.at[h, dy, dk])
        for i in range(6):
            done(bb.at[0, 0, 0], b2s.at[h, i])
        for to in range(2):
            done(zrel.at[0, 0], zls.at[h, to])
            for half in range(2):
                done(zrel.at[0, 0], dbs.at[h, to, half])
    for dy, dk in ((1, 0), (1, 1), (0, 1)):
        done(slr.at[0], lrs.at[dy, dk])

    @pl.when(a != b)
    def _():
        for h in range(2):
            done(sbb.at[0, 0], b1s.at[h, 0, 0])
            done(sbb.at[0, 0], d1s.at[h, 0, 0])


def body(query_proj, key_proj, value_proj, out_grad, pair_bias, log_sum_exp, correction, pad_mask):
    vmem = pl.BlockSpec(memory_space=pltpu.VMEM)
    f = lambda *shape: pltpu.VMEM(shape, F32)
    dma = lambda *shape: pltpu.SemaphoreType.DMA(shape)
    swap = lambda y: jnp.transpose(y, (1, 0, 2))
    pair = [dma(2, 2, 2)] * 2
    dq, dk, dv, db = pl.pallas_call(
        kernel,
        out_shape=[jax.ShapeDtypeStruct((5, 256, 128), F32)] * 3
        + [jax.ShapeDtypeStruct((4, 128, 256), F32)],
        in_specs=[vmem] * 8,
        out_specs=[vmem] * 4,
        scratch_shapes=[
            f(2, 2, 2, 5, 32, 256),
            f(2, 2, 2, 5, 32, 256),
            f(2, 2, 128, 256),
            f(2, 2, 2, 5, 256),
            f(2, 4, 2, 2, 5, 32, 256),
            f(2, 2, 2, 2, 5, 32, 256),
            f(2, 2, 2, 2, 5, 256),
            f(2, 4, 2, 2, 128, 256),
            f(2, 4, 2, 2, 5, 32, 256),
            f(2, 4, 2, 2, 5, 32, 256),
            f(2, 2, 2, 5, 32, 256),
            f(2, 2, 2, 128, 256),
            f(2, 2, 2, 5, 32, 256),
            f(2, 2, 2, 5, 32, 256),
            f(2, 4, 2, 2, 128, 256),
            f(2, 2, 2, 2, 128, 256),
            f(2, 2, 2, 128, 256),
            pltpu.VMEM((2, 2, 5, 128, 512), BF),
            pltpu.VMEM((2, 2, 5, 128, 512), BF),
            pltpu.VMEM((2, 4, 256, 512), BF),
            dma(2, 7), dma(2, 4, 2), *pair, dma(2, 2), dma(2, 2), *pair, dma(2, 6), dma(2, 4, 2),
            dma(2, 4, 2), dma(2, 4, 2), dma(2, 2), dma(2, 2), *pair, dma(2, 2), dma(2, 2), dma(2, 2, 2), dma(2, 2, 2), *pair,
        ],
        compiler_params=pltpu.CompilerParams(
            collective_id=0, has_side_effects=True, vmem_limit_bytes=60 * 2**20
        ),
    )(
        swap(query_proj), swap(key_proj), swap(value_proj), swap(out_grad), pair_bias,
        swap(log_sum_exp), swap(correction), pad_mask.reshape(16, 128),
    )
    return swap(dq), swap(dk), swap(dv), db


def solution(mesh):
    return jax.shard_map(
        body,
        mesh=mesh,
        in_specs=(
            P("col", "row", None),
            P("col", "row", None),
            P("col", "row", None),
            P("col", "row", None),
            P(None, "row", "col"),
            P(None, "row", "col"),
            P(None, "row", "col"),
            P(),
        ),
        out_specs=(
            P("col", "row", None),
            P("col", "row", None),
            P("col", "row", None),
            P(None, "row", "col"),
        ),
        check_vma=False,
    )
```

```python
import functools
import math

import jax
import jax.numpy as jnp
from jax import lax
from jax.experimental import pallas as pl
from jax.experimental.pallas import tpu as pltpu
from jax.sharding import PartitionSpec as P

LOG2E = math.log2(math.e)
ROOT = 1.0 / math.sqrt(32)
BF = jnp.bfloat16
F32 = jnp.float32
MESH = pl.DeviceIdType.MESH


def place(z, a, k, x, b):
    return (z * 4 + a * 2 + k, x * 2 + b)


def dg(lhs, rhs, lhs_dim, rhs_dim):
    return lax.dot_general(
        lhs, rhs, (((lhs_dim,), (rhs_dim,)), ((), ())), preferred_element_type=F32
    )


def split(x):
    hi = x.astype(BF)
    return hi, (x - hi.astype(F32)).astype(BF)


def extra_rows(x):
    hi = x.astype(BF)
    rest = x - hi.astype(F32)
    mid = rest.astype(BF)
    low = (rest - mid.astype(F32)).astype(BF)
    row = lax.broadcasted_iota(jnp.int32, (32, x.shape[1]), 0)
    out = jnp.where(
        row == 0,
        hi.astype(F32),
        jnp.where(row == 1, mid.astype(F32), jnp.where(row == 2, low.astype(F32), 0.0)),
    )
    return out.astype(BF)


def key_rows(x):
    hi, low = split(x)
    ones = jnp.ones((32, x.shape[1]), BF)
    return hi, low, jnp.concatenate([hi, low, hi, ones], axis=0)


def pack_queries(h, qgb, lrb, qp, gp):
    def step(j, carry):
        for src in range(2):
            for half in range(2):
                cols = slice(256 * half, 256 * half + 256)
                level = lrb[half, src, 0, h, pl.ds(j, 1), :] * (-LOG2E)
                corr = -lrb[half, src, 1, h, pl.ds(j, 1), :]
                for which, packed, scale, row in (
                    (0, qp, LOG2E * ROOT, level),
                    (1, gp, None, corr),
                ):
                    x = qgb[h, half, src, which, j]
                    hi, low = split(x if scale is None else x * scale)
                    packed[h, src, j, 0:32, cols] = hi
                    packed[h, src, j, 32:64, cols] = hi
                    packed[h, src, j, 64:96, cols] = low
                    packed[h, src, j, 96:128, cols] = extra_rows(row)
        return carry

    lax.fori_loop(0, 5, step, 0)


def compute_block(kv, qp, gp, bias, dkv, dqb, db, scr, first):
    for half in range(2):
        for part in range(2):
            db[half, part] = jnp.zeros((128, 256), F32)

    def column(j):
        keys = [None, None]
        scores = [None, None]
        grads = [None, None]
        for src in range(2):
            k_hi, k_low, kp = key_rows(kv[src, 0, j])
            _, _, vp = key_rows(kv[src, 1, j])
            keys[src] = (k_hi, k_low)
            scores[src] = dg(kp, qp[src, j], 0, 0)
            grads[src] = dg(vp, gp[src, j], 0, 0)
        for src in range(2):
            w_hi, w_low, s_hi, s_low = [scr.at[2 * (j % 2) + src, i] for i in range(4)]
            for half in range(2):
                cols = slice(256 * half, 256 * half + 256)
                for part in range(2):
                    rows = slice(128 * part, 128 * part + 128)
                    w = jnp.exp2(scores[src][rows, cols] + bias[half, part])
                    ds = w * grads[src][rows, cols]
                    db[half, part] += ds
                    w_hi[rows, cols], w_low[rows, cols] = split(w)
                    s_hi[rows, cols], s_low[rows, cols] = split(ds)
        for src in range(2):
            w_hi, w_low, s_hi, s_low = [scr.at[2 * (j % 2) + src, i] for i in range(4)]
            k_hi, k_low = keys[src]
            r = dg(jnp.concatenate([k_hi, k_low], axis=0), s_hi[...], 1, 0)
            total = (r[:32] + r[32:] + dg(k_hi, s_low[...], 1, 0)) * ROOT
            for half in range(2):
                mine = total[:, 256 * half : 256 * half + 256]
                dqb[half, src, j] = jnp.where(first, mine, dqb[half, src, j] + mine)
            r = dg(qp[src, j, 32:96, :], s_hi[...], 1, 1)
            r2 = dg(qp[src, j, 0:32, :], s_low[...], 1, 1)
            dkv[src, 0, j] = (r[:32] + r[32:] + r2) * (1.0 / LOG2E)
            r = dg(gp[src, j, 32:96, :], w_hi[...], 1, 1)
            r2 = dg(gp[src, j, 0:32, :], w_low[...], 1, 1)
            dkv[src, 1, j] = r[:32] + r[32:] + r2

    for j in range(5):
        column(j)


def kernel(
    q_ref, k_ref, v_ref, g_ref, b_ref, l_ref, r_ref, m_ref,
    dq_ref, dk_ref, dv_ref, db_ref,
    skv, sqg, sbb, slr, kvb, qgb, lrb, bb, dkv, rkv, rel, zrel, dqb, rdq, dbb, rb, rbb, qp, gp, scr,
    kvs, kvr, qgs, qgr, lrs, lrr, b1s, b1r, b2s, b2r, dks, dkr, rls, rlr, dqs, dqr, zls, zlr, dbs, dbr, d1s, d1r,
):
    row = lax.axis_index("row")
    col = lax.axis_index("col")
    z = row // 4
    a = (row // 2) % 2
    k = row % 2
    x = col // 2
    b = col % 2
    right, left = (x + 1) % 4, (x + 3) % 4
    up, down = (z + 1) % 4, (z + 3) % 4

    def at(dz=0, dx=0, dk=0):
        return place((z + dz) % 4, a, (k + dk) % 2, (x + dx) % 4, b)

    barrier = pltpu.get_barrier_semaphore()
    partners = [at(dx=dx, dk=dk) for dx in (1, 3) for dk in (0, 1)]
    partners += [at(dz=dz) for dz in (1, 3)]
    for da in (0, 1):
        for dy in (0, 1):
            for dk in (0, 1):
                if da or dy or dk:
                    partners.append(place(z, (a + da) % 2, (k + dk) % 2, x, (b + dy) % 2))
    for partner in partners:
        pl.semaphore_signal(barrier, inc=1, device_id=partner, device_id_type=MESH)

    def remote(src, dst, send, recv, target):
        return pltpu.make_async_remote_copy(
            src_ref=src, dst_ref=dst, send_sem=send, recv_sem=recv,
            device_id=target, device_id_type=MESH,
        )

    def done(ref, sem):
        pltpu.make_async_copy(ref, ref, sem).wait()

    def turn(ref, dst, which):
        for j in range(5):
            t = ref[j].T
            for d in range(2):
                for h in range(2):
                    first = 64 * d + 32 * h
                    dst[h, d, which, j] = t[first : first + 32]

    def send_bias(h):
        for da in (0, 1):
            for dk in (0, 1):
                a_to = (a + da) % 2
                d = (k + dk) % 2
                copy = remote(
                    sbb.at[h, d], bb.at[h, z, b, k], b1s.at[h, da, dk], b1r.at[h, b, k],
                    place(z, a_to, d, x, a),
                )
                if da == 0 and dk == 0:
                    own = pltpu.make_async_copy(sbb.at[h, k], bb.at[h, z, b, k], b1r.at[h, b, k])
                    pl.when(a == b)(own.start)
                    pl.when(a != b)(copy.start)
                else:
                    copy.start()

    def spread_bias(h):
        for half in range(2):
            for part in range(2):
                done(bb.at[h, z, half, part], b1r.at[h, half, part])
        for i, (to, half) in enumerate(((1, 0), (3, 1), (1, 1), (3, 0))):
            remote(
                bb.at[h, z, half], bb.at[h, z, half], b2s.at[h, i], b2r.at[h, z, half], at(dz=to)
            ).start()

    def pass_bias(h):
        done(bb.at[h, down, 0], b2r.at[h, down, 0])
        remote(
            bb.at[h, down, 0], bb.at[h, down, 0], b2s.at[h, 4], b2r.at[h, down, 0], at(dz=1)
        ).start()
        done(bb.at[h, up, 1], b2r.at[h, up, 1])
        remote(
            bb.at[h, up, 1], bb.at[h, up, 1], b2s.at[h, 5], b2r.at[h, up, 1], at(dz=3)
        ).start()

    def wait_bias(h, zk):
        def rest(half):
            passed = (half == 0) & (zk == down) | (half == 1) & (zk == up)
            pl.when((zk != z) & jnp.logical_not(passed))(
                lambda: done(bb.at[h, zk, half], b2r.at[h, zk, half])
            )

        rest(0)
        rest(1)

    def send_keys(h):
        pltpu.make_async_copy(skv.at[h, k], kvb.at[h, x, k], kvr.at[h, x, k]).start()
        for i, (dx, dk) in enumerate(((1, 0), (3, 0), (1, 1), (3, 1), (0, 1))):
            remote(
                skv.at[h, (k + dk) % 2], kvb.at[h, x, k], kvs.at[h, i], kvr.at[h, x, k],
                at(dx=dx, dk=dk),
            ).start()

    def pass_keys(h):
        done(kvb.at[h, left, 0], kvr.at[h, left, 0])
        remote(
            kvb.at[h, left, 0], kvb.at[h, left, 0], kvs.at[h, 5], kvr.at[h, left, 0], at(dx=1)
        ).start()
        done(kvb.at[h, right, 1], kvr.at[h, right, 1])
        remote(
            kvb.at[h, right, 1], kvb.at[h, right, 1], kvs.at[h, 6], kvr.at[h, right, 1], at(dx=3)
        ).start()

    def wait_keys(h, xk):
        pl.when(xk != left)(lambda: done(kvb.at[h, xk, 0], kvr.at[h, xk, 0]))
        pl.when(xk != right)(lambda: done(kvb.at[h, xk, 1], kvr.at[h, xk, 1]))

    def send_queries(h):
        pltpu.make_async_copy(sqg.at[h, k], qgb.at[h, b, k], qgr.at[h, b, k]).start()
        for dy, dk in ((1, 0), (1, 1), (0, 1)):
            d = (k + dk) % 2
            remote(
                sqg.at[h, d], qgb.at[h, b, k], qgs.at[h, dy, dk], qgr.at[h, b, k],
                place(z, a, d, x, (b + dy) % 2),
            ).start()

    def wait_queries(h):
        for half in range(2):
            for src in range(2):
                done(qgb.at[h, half, src], qgr.at[h, half, src])

    def push_bias_grad(h, to, half):
        zk = (up, down)[to]
        remote(
            dbb.at[h, zk, half], rb.at[h, to, half], dbs.at[h, to, half], dbr.at[h, to, half],
            place(zk, a, k, x, b),
        ).start()

    def send_bias_grad(h, zk):
        @pl.when(zk == (z + 2) % 4)
        def _():
            for half, dz in ((0, 1), (1, 3)):
                remote(
                    dbb.at[h, zk, half], zrel.at[h, half], zls.at[h, half], zlr.at[h, half],
                    at(dz=dz),
                ).start()

        pl.when(zk == up)(lambda: push_bias_grad(h, 0, 1))
        pl.when(zk == down)(lambda: push_bias_grad(h, 1, 0))

    def finish_bias_grad(h, zk):
        def finish(to):
            half = to
            done(zrel.at[h, half], zlr.at[h, half])
            for part in range(2):
                dbb[h, zk, half, part] += zrel[h, half, part]
            push_bias_grad(h, to, half)

        pl.when(zk == up)(lambda: finish(0))
        pl.when(zk == down)(lambda: finish(1))

    def sum_bias(h):
        for to in range(2):
            for half in range(2):
                done(rb.at[h, to, half], dbr.at[h, to, half])
        for half in range(2):
            for part in range(2):
                dbb[h, z, half, part] += rb[h, 0, half, part] + rb[h, 1, half, part]
        for dy in (1, 0):
            for dk in (0, 1):
                half = (b + dy) % 2
                part = (k + dk) % 2
                copy = remote(
                    dbb.at[h, z, half, part], rbb.at[h, a, k], d1s.at[h, dy, dk], d1r.at[h, a, k],
                    place(z, b, part, x, half),
                )
                if dy == 0 and dk == 0:
                    own = pltpu.make_async_copy(dbb.at[h, z, b, k], rbb.at[h, a, k], d1r.at[h, a, k])
                    pl.when(a == b)(own.start)
                    pl.when(a != b)(copy.start)
                else:
                    copy.start()

    def send_key_grads(h, xk, d):
        remote(
            dkv.at[h, xk, d], rkv.at[h, x, k], dks.at[h, xk, d], dkr.at[h, x, k],
            place(z, a, d, xk, b),
        ).start()

    def add_passed(h, xk, d):
        done(rel.at[h, d], rlr.at[h, d])
        for which in range(2):
            for j in range(5):
                dkv[h, xk, d, which, j] += rel[h, d, which, j]

    def send_query_grads(h):
        for dy, dk in ((1, 0), (1, 1), (0, 1)):
            d = (k + dk) % 2
            to = (b + dy) % 2
            remote(
                dqb.at[h, to, d], rdq.at[h, b, k], dqs.at[h, dy, dk], dqr.at[h, b, k],
                place(z, a, d, x, to),
            ).start()

    alive = jnp.broadcast_to(m_ref[pl.ds(row, 1), :], (128, 128)).astype(F32).T
    alive = jnp.concatenate([alive, alive], axis=1) == 1.0
    for h in range(4):
        sbb[h % 2, h // 2] = jnp.where(alive, b_ref[h] * LOG2E, -1e30)
    for d in range(2):
        for h in range(2):
            slr[d, 0, h] = l_ref[:, 2 * d + h, :]
            slr[d, 1, h] = r_ref[:, 2 * d + h, :]

    pl.semaphore_wait(barrier, len(partners))

    send_bias(0)
    turn(k_ref, skv, 0)
    turn(v_ref, skv, 1)
    send_keys(0)
    pltpu.make_async_copy(slr.at[k], lrb.at[b, k], lrr.at[b, k]).start()
    for dy, dk in ((1, 0), (1, 1), (0, 1)):
        d = (k + dk) % 2
        remote(
            slr.at[d], lrb.at[b, k], lrs.at[dy, dk], lrr.at[b, k], place(z, a, d, x, (b + dy) % 2)
        ).start()
    turn(q_ref, sqg, 0)
    turn(g_ref, sqg, 1)
    send_queries(0)
    spread_bias(0)
    pass_keys(0)
    send_keys(1)
    pass_bias(0)
    for half in range(2):
        for src in range(2):
            done(lrb.at[half, src], lrr.at[half, src])
    wait_queries(0)
    send_bias(1)
    pack_queries(0, qgb, lrb, qp, gp)

    def block_of(t):
        return (x + 2 + 3 * t + 3 * (t // 2) + 2 * (t // 3)) % 4

    def block(n, carry):
        h = n // 4
        t = n % 4
        xk = block_of(t)

        @pl.when(n == 4)
        def _():
            wait_queries(1)
            pack_queries(1, qgb, lrb, qp, gp)

        wait_keys(h, xk)
        wait_bias(h, xk)
        compute_block(
            kvb.at[h, xk], qp.at[h], gp.at[h], bb.at[h, xk], dkv.at[h, xk], dqb.at[h],
            dbb.at[h, xk], scr, t == 0,
        )
        send_bias_grad(h, xk)
        pl.when(t == 3)(lambda: send_query_grads(h))

        @pl.when(t == 0)
        def _():
            for d, dx in ((0, 1), (1, 3)):
                remote(
                    dkv.at[h, xk, d], rel.at[h, d], rls.at[h, d], rlr.at[h, d], at(dx=dx)
                ).start()

        @pl.when(t == 1)
        def _():
            send_key_grads(h, right, 1)

        @pl.when(t == 2)
        def _():
            add_passed(h, right, 0)
            send_key_grads(h, right, 0)
            send_key_grads(h, left, 0)

        @pl.when(t == 3)
        def _():
            send_key_grads(h, x, 1 - k)
            add_passed(h, left, 1)
            send_key_grads(h, left, 1)

        @pl.when(n > 0)
        def _():
            finish_bias_grad((n - 1) // 4, block_of((n - 1) % 4))

        @pl.when(n == 0)
        def _():
            spread_bias(1)
            send_queries(1)

        @pl.when(n == 1)
        def _():
            pass_keys(1)

        @pl.when(n == 2)
        def _():
            pass_bias(1)

        @pl.when(n == 6)
        def _():
            sum_bias(0)

        return carry

    lax.fori_loop(0, 8, block, 0)
    finish_bias_grad(1, x)

    for h in range(2):
        done(rkv.at[h, x, 1 - k], dkr.at[h, x, 1 - k])
        for xk in (right, left):
            for c in range(2):
                done(rkv.at[h, xk, c], dkr.at[h, xk, c])

    def join(own, other):
        low = jnp.where(k == 0, own, other)
        high = jnp.where(k == 0, other, own)
        return jnp.concatenate([low, high], axis=0).T

    def rows(ref, *index):
        return jnp.concatenate([ref[(0, *index)], ref[(1, *index)]], axis=0)

    for j in range(5):
        for which, out in ((0, dk_ref), (1, dv_ref)):
            own = rows(dkv, x, k, which, j)
            other = rows(rkv, x, 1 - k, which, j)
            for xk in (right, left):
                own = own + rows(rkv, xk, k, which, j)
                other = other + rows(rkv, xk, 1 - k, which, j)
            out[j] = join(own, other)
    sum_bias(1)
    for h in range(2):
        for dy, dk in ((1, 0), (1, 1), (0, 1)):
            done(rdq.at[h, (b + dy) % 2, (k + dk) % 2], dqr.at[h, (b + dy) % 2, (k + dk) % 2])
    for j in range(5):
        own = rows(dqb, b, k, j) + rows(rdq, 1 - b, k, j)
        other = rows(rdq, 0, 1 - k, j) + rows(rdq, 1, 1 - k, j)
        dq_ref[j] = join(own, other)
    for h in range(2):
        for half in range(2):
            for part in range(2):
                done(rbb.at[h, half, part], d1r.at[h, half, part])
        for d in range(2):
            db_ref[2 * d + h] = rbb[h, 0, d] + rbb[h, 1, d]

    for h in range(2):
        for i in range(7):
            done(skv.at[0, 0], kvs.at[h, i])
        done(dkv.at[0, 0, 0], dks.at[h, x, 1 - k])
        for d in range(2):
            done(dkv.at[0, 0, 0], dks.at[h, right, d])
            done(dkv.at[0, 0, 0], dks.at[h, left, d])
            done(rel.at[0, 0], rls.at[h, d])
        for dy, dk in ((1, 0), (1, 1), (0, 1)):
            done(sqg.at[0, 0], qgs.at[h, dy, dk])
            done(dqb.at[0, 0, 0], dqs.at[h, dy, dk])
            done(sbb.at[0, 0], b1s.at[h, dy, dk])
            done(sbb.at[0, 0], d1s.at[h, dy, dk])
        for i in range(6):
            done(bb.at[0, 0, 0], b2s.at[h, i])
        for to in range(2):
            done(zrel.at[0, 0], zls.at[h, to])
            for half in range(2):
                done(zrel.at[0, 0], dbs.at[h, to, half])
    for dy, dk in ((1, 0), (1, 1), (0, 1)):
        done(slr.at[0], lrs.at[dy, dk])

    @pl.when(a != b)
    def _():
        for h in range(2):
            done(sbb.at[0, 0], b1s.at[h, 0, 0])
            done(sbb.at[0, 0], d1s.at[h, 0, 0])


def hand_over(*refs):
    for i in range(4):
        refs[4 + i][...] = refs[i][...]


def body(query_proj, key_proj, value_proj, out_grad, pair_bias, log_sum_exp, correction, pad_mask):
    vmem = pl.BlockSpec(memory_space=pltpu.VMEM)
    f = lambda *shape: pltpu.VMEM(shape, F32)
    dma = lambda *shape: pltpu.SemaphoreType.DMA(shape)
    swap = lambda y: jnp.transpose(y, (1, 0, 2))
    pair = [dma(2, 2, 2)] * 2
    dq, dk, dv, db = pl.pallas_call(
        kernel,
        out_shape=[jax.ShapeDtypeStruct((5, 256, 128), F32)] * 3
        + [jax.ShapeDtypeStruct((4, 128, 256), F32)],
        in_specs=[vmem] * 8,
        out_specs=[vmem] * 4,
        scratch_shapes=[
            f(2, 2, 2, 5, 32, 256),
            f(2, 2, 2, 5, 32, 256),
            f(2, 2, 128, 256),
            f(2, 2, 2, 5, 256),
            f(2, 4, 2, 2, 5, 32, 256),
            f(2, 2, 2, 2, 5, 32, 256),
            f(2, 2, 2, 2, 5, 256),
            f(2, 4, 2, 2, 128, 256),
            f(2, 4, 2, 2, 5, 32, 256),
            f(2, 4, 2, 2, 5, 32, 256),
            f(2, 2, 2, 5, 32, 256),
            f(2, 2, 2, 128, 256),
            f(2, 2, 2, 5, 32, 256),
            f(2, 2, 2, 5, 32, 256),
            f(2, 4, 2, 2, 128, 256),
            f(2, 2, 2, 2, 128, 256),
            f(2, 2, 2, 128, 256),
            pltpu.VMEM((2, 2, 5, 128, 512), BF),
            pltpu.VMEM((2, 2, 5, 128, 512), BF),
            pltpu.VMEM((4, 4, 256, 512), BF),
            dma(2, 7), dma(2, 4, 2), *pair, dma(2, 2), dma(2, 2), *pair, dma(2, 6), dma(2, 4, 2),
            dma(2, 4, 2), dma(2, 4, 2), dma(2, 2), dma(2, 2), *pair, dma(2, 2), dma(2, 2), dma(2, 2, 2), dma(2, 2, 2), *pair,
        ],
        compiler_params=pltpu.CompilerParams(
            collective_id=0, has_side_effects=True, vmem_limit_bytes=60 * 2**20
        ),
    )(
        swap(query_proj), swap(key_proj), swap(value_proj), swap(out_grad), pair_bias,
        swap(log_sum_exp), swap(correction), pad_mask.reshape(16, 128),
    )
    flat = lambda y: y.reshape(1280, 128)
    rows = pl.BlockSpec((320, 128), lambda i: (i, 0))
    plane = pl.BlockSpec((1, 128, 256), lambda i: (i, 0, 0))
    dq, dk, dv, db = pl.pallas_call(
        hand_over,
        grid=(4,),
        out_shape=[jax.ShapeDtypeStruct((1280, 128), F32)] * 3
        + [jax.ShapeDtypeStruct((4, 128, 256), F32)],
        in_specs=[rows] * 3 + [plane],
        out_specs=[rows] * 3 + [plane],
    )(flat(dq), flat(dk), flat(dv), db)
    whole = lambda y: swap(y.reshape(5, 256, 128))
    return whole(dq), whole(dk), whole(dv), db


def solution(mesh):
    return jax.shard_map(
        body,
        mesh=mesh,
        in_specs=(
            P("col", "row", None),
            P("col", "row", None),
            P("col", "row", None),
            P("col", "row", None),
            P(None, "row", "col"),
            P(None, "row", "col"),
            P(None, "row", "col"),
            P(),
        ),
        out_specs=(
            P("col", "row", None),
            P("col", "row", None),
            P("col", "row", None),
            P(None, "row", "col"),
        ),
        check_vma=False,
    )
```

```python
import functools
import math

import jax
import jax.numpy as jnp
from jax import lax
from jax.experimental import pallas as pl
from jax.experimental.pallas import tpu as pltpu
from jax.sharding import PartitionSpec as P

LOG2E = math.log2(math.e)
ROOT = 1.0 / math.sqrt(32)
BF = jnp.bfloat16
F32 = jnp.float32
MESH = pl.DeviceIdType.MESH


def place(z, a, k, x, b):
    return (z * 4 + a * 2 + k, x * 2 + b)


def dg(lhs, rhs, lhs_dim, rhs_dim):
    return lax.dot_general(
        lhs, rhs, (((lhs_dim,), (rhs_dim,)), ((), ())), preferred_element_type=F32
    )


def split(x):
    hi = x.astype(BF)
    return hi, (x - hi.astype(F32)).astype(BF)


def extra_rows(x):
    hi = x.astype(BF)
    rest = x - hi.astype(F32)
    mid = rest.astype(BF)
    low = (rest - mid.astype(F32)).astype(BF)
    row = lax.broadcasted_iota(jnp.int32, (32, x.shape[1]), 0)
    out = jnp.where(
        row == 0,
        hi.astype(F32),
        jnp.where(row == 1, mid.astype(F32), jnp.where(row == 2, low.astype(F32), 0.0)),
    )
    return out.astype(BF)


def key_rows(x):
    hi, low = split(x)
    ones = jnp.ones((32, x.shape[1]), BF)
    return hi, low, jnp.concatenate([hi, low, hi, ones], axis=0)


def pack_queries(h, half, qgb, lrb, qp, gp):
    cols = pl.ds(pl.multiple_of(256 * half, 256), 256)

    def step(j, carry):
        for src in range(2):
            level = lrb[half, src, 0, h, pl.ds(j, 1), :] * (-LOG2E)
            corr = -lrb[half, src, 1, h, pl.ds(j, 1), :]
            for which, packed, scale, row in (
                (0, qp, LOG2E * ROOT, level),
                (1, gp, None, corr),
            ):
                x = qgb[h, half, src, which, j]
                hi, low = split(x if scale is None else x * scale)
                packed[h, src, j, 0:32, cols] = hi
                packed[h, src, j, 32:64, cols] = hi
                packed[h, src, j, 64:96, cols] = low
                packed[h, src, j, 96:128, cols] = extra_rows(row)
        return carry

    lax.fori_loop(0, 5, step, 0)


def compute_block(kv, qp, gp, bias, dkv, dqb, db, scr, first):
    for half in range(2):
        for part in range(2):
            db[half, part] = jnp.zeros((128, 256), F32)

    def column(j):
        keys = [None, None]
        scores = [None, None]
        grads = [None, None]
        for src in range(2):
            k_hi, k_low, kp = key_rows(kv[src, 0, j])
            _, _, vp = key_rows(kv[src, 1, j])
            keys[src] = (k_hi, k_low)
            scores[src] = dg(kp, qp[src, j], 0, 0)
            grads[src] = dg(vp, gp[src, j], 0, 0)
        for src in range(2):
            w_hi, w_low, s_hi, s_low = [scr.at[2 * (j % 2) + src, i] for i in range(4)]
            for half in range(2):
                cols = slice(256 * half, 256 * half + 256)
                for part in range(2):
                    rows = slice(128 * part, 128 * part + 128)
                    w = jnp.exp2(scores[src][rows, cols] + bias[half, part])
                    ds = w * grads[src][rows, cols]
                    db[half, part] += ds
                    w_hi[rows, cols], w_low[rows, cols] = split(w)
                    s_hi[rows, cols], s_low[rows, cols] = split(ds)
        for src in range(2):
            w_hi, w_low, s_hi, s_low = [scr.at[2 * (j % 2) + src, i] for i in range(4)]
            k_hi, k_low = keys[src]
            r = dg(jnp.concatenate([k_hi, k_low], axis=0), s_hi[...], 1, 0)
            total = (r[:32] + r[32:] + dg(k_hi, s_low[...], 1, 0)) * ROOT
            for half in range(2):
                mine = total[:, 256 * half : 256 * half + 256]
                dqb[half, src, j] = jnp.where(first, mine, dqb[half, src, j] + mine)
            r = dg(qp[src, j, 32:96, :], s_hi[...], 1, 1)
            r2 = dg(qp[src, j, 0:32, :], s_low[...], 1, 1)
            dkv[src, 0, j] = (r[:32] + r[32:] + r2) * (1.0 / LOG2E)
            r = dg(gp[src, j, 32:96, :], w_hi[...], 1, 1)
            r2 = dg(gp[src, j, 0:32, :], w_low[...], 1, 1)
            dkv[src, 1, j] = r[:32] + r[32:] + r2

    for j in range(5):
        column(j)


def kernel(
    q_ref, k_ref, v_ref, g_ref, b_ref, l_ref, r_ref, m_ref,
    dq_ref, dk_ref, dv_ref, db_ref,
    skv, sqg, sbb, slr, kvb, qgb, lrb, bb, dkv, rkv, rel, zrel, dqb, rdq, dbb, rb, rbb, qp, gp, scr,
    kvs, kvr, qgs, qgr, lrs, lrr, b1s, b1r, b2s, b2r, dks, dkr, rls, rlr, dqs, dqr, zls, zlr, dbs, dbr, d1s, d1r,
):
    row = lax.axis_index("row")
    col = lax.axis_index("col")
    z = row // 4
    a = (row // 2) % 2
    k = row % 2
    x = col // 2
    b = col % 2
    right, left = (x + 1) % 4, (x + 3) % 4
    up, down = (z + 1) % 4, (z + 3) % 4

    def at(dz=0, dx=0, dk=0):
        return place((z + dz) % 4, a, (k + dk) % 2, (x + dx) % 4, b)

    barrier = pltpu.get_barrier_semaphore()
    partners = [at(dx=dx, dk=dk) for dx in (1, 3) for dk in (0, 1)]
    partners += [at(dz=dz) for dz in (1, 3)]
    for da in (0, 1):
        for dy in (0, 1):
            for dk in (0, 1):
                if da or dy or dk:
                    partners.append(place(z, (a + da) % 2, (k + dk) % 2, x, (b + dy) % 2))
    for partner in partners:
        pl.semaphore_signal(barrier, inc=1, device_id=partner, device_id_type=MESH)

    def remote(src, dst, send, recv, target):
        return pltpu.make_async_remote_copy(
            src_ref=src, dst_ref=dst, send_sem=send, recv_sem=recv,
            device_id=target, device_id_type=MESH,
        )

    def done(ref, sem):
        pltpu.make_async_copy(ref, ref, sem).wait()

    def turn(ref, dst, which):
        for j in range(5):
            t = ref[j].T
            for d in range(2):
                for h in range(2):
                    first = 64 * d + 32 * h
                    dst[h, d, which, j] = t[first : first + 32]

    def send_bias(h):
        for da in (0, 1):
            for dk in (0, 1):
                a_to = (a + da) % 2
                d = (k + dk) % 2
                copy = remote(
                    sbb.at[h, d], bb.at[h, z, b, k], b1s.at[h, da, dk], b1r.at[h, b, k],
                    place(z, a_to, d, x, a),
                )
                if da == 0 and dk == 0:
                    own = pltpu.make_async_copy(sbb.at[h, k], bb.at[h, z, b, k], b1r.at[h, b, k])
                    pl.when(a == b)(own.start)
                    pl.when(a != b)(copy.start)
                else:
                    copy.start()

    def spread_bias(h):
        for half in range(2):
            for part in range(2):
                done(bb.at[h, z, half, part], b1r.at[h, half, part])
        for i, (to, half) in enumerate(((1, 0), (3, 1), (1, 1), (3, 0))):
            remote(
                bb.at[h, z, half], bb.at[h, z, half], b2s.at[h, i], b2r.at[h, z, half], at(dz=to)
            ).start()

    def pass_bias(h):
        done(bb.at[h, down, 0], b2r.at[h, down, 0])
        remote(
            bb.at[h, down, 0], bb.at[h, down, 0], b2s.at[h, 4], b2r.at[h, down, 0], at(dz=1)
        ).start()
        done(bb.at[h, up, 1], b2r.at[h, up, 1])
        remote(
            bb.at[h, up, 1], bb.at[h, up, 1], b2s.at[h, 5], b2r.at[h, up, 1], at(dz=3)
        ).start()

    def wait_bias(h, zk):
        def rest(half):
            passed = (half == 0) & (zk == down) | (half == 1) & (zk == up)
            pl.when((zk != z) & jnp.logical_not(passed))(
                lambda: done(bb.at[h, zk, half], b2r.at[h, zk, half])
            )

        rest(0)
        rest(1)

    def send_keys(h):
        pltpu.make_async_copy(skv.at[h, k], kvb.at[h, x, k], kvr.at[h, x, k]).start()
        for i, (dx, dk) in enumerate(((1, 0), (3, 0), (1, 1), (3, 1), (0, 1))):
            remote(
                skv.at[h, (k + dk) % 2], kvb.at[h, x, k], kvs.at[h, i], kvr.at[h, x, k],
                at(dx=dx, dk=dk),
            ).start()

    def pass_keys(h):
        done(kvb.at[h, left, 0], kvr.at[h, left, 0])
        remote(
            kvb.at[h, left, 0], kvb.at[h, left, 0], kvs.at[h, 5], kvr.at[h, left, 0], at(dx=1)
        ).start()
        done(kvb.at[h, right, 1], kvr.at[h, right, 1])
        remote(
            kvb.at[h, right, 1], kvb.at[h, right, 1], kvs.at[h, 6], kvr.at[h, right, 1], at(dx=3)
        ).start()

    def wait_keys(h, xk):
        pl.when(xk != left)(lambda: done(kvb.at[h, xk, 0], kvr.at[h, xk, 0]))
        pl.when(xk != right)(lambda: done(kvb.at[h, xk, 1], kvr.at[h, xk, 1]))

    def share_queries(h):
        pltpu.make_async_copy(sqg.at[h, k], qgb.at[h, b, k], qgr.at[h, b, k]).start()
        push_queries(h, ((0, 1),))

    def send_queries(h):
        push_queries(h, ((1, 0), (1, 1)))

    def push_queries(h, steps):
        for dy, dk in steps:
            d = (k + dk) % 2
            remote(
                sqg.at[h, d], qgb.at[h, b, k], qgs.at[h, dy, dk], qgr.at[h, b, k],
                place(z, a, d, x, (b + dy) % 2),
            ).start()

    def take_queries(h, half):
        for src in range(2):
            done(qgb.at[h, half, src], qgr.at[h, half, src])
        pack_queries(h, half, qgb, lrb, qp, gp)

    def wait_levels(half):
        for src in range(2):
            done(lrb.at[half, src], lrr.at[half, src])

    def push_bias_grad(h, to, half):
        zk = (up, down)[to]
        remote(
            dbb.at[h, zk, half], rb.at[h, to, half], dbs.at[h, to, half], dbr.at[h, to, half],
            place(zk, a, k, x, b),
        ).start()

    def send_bias_grad(h, zk):
        @pl.when(zk == (z + 2) % 4)
        def _():
            for half, dz in ((0, 1), (1, 3)):
                remote(
                    dbb.at[h, zk, half], zrel.at[h, half], zls.at[h, half], zlr.at[h, half],
                    at(dz=dz),
                ).start()

        pl.when(zk == up)(lambda: push_bias_grad(h, 0, 1))
        pl.when(zk == down)(lambda: push_bias_grad(h, 1, 0))

    def finish_bias_grad(h, zk):
        def finish(to):
            half = to
            done(zrel.at[h, half], zlr.at[h, half])
            for part in range(2):
                dbb[h, zk, half, part] += zrel[h, half, part]
            push_bias_grad(h, to, half)

        pl.when(zk == up)(lambda: finish(0))
        pl.when(zk == down)(lambda: finish(1))

    def sum_bias(h):
        for to in range(2):
            for half in range(2):
                done(rb.at[h, to, half], dbr.at[h, to, half])
        for half in range(2):
            for part in range(2):
                dbb[h, z, half, part] += rb[h, 0, half, part] + rb[h, 1, half, part]
        for dy in (1, 0):
            for dk in (0, 1):
                half = (b + dy) % 2
                part = (k + dk) % 2
                copy = remote(
                    dbb.at[h, z, half, part], rbb.at[h, a, k], d1s.at[h, dy, dk], d1r.at[h, a, k],
                    place(z, b, part, x, half),
                )
                if dy == 0 and dk == 0:
                    own = pltpu.make_async_copy(dbb.at[h, z, b, k], rbb.at[h, a, k], d1r.at[h, a, k])
                    pl.when(a == b)(own.start)
                    pl.when(a != b)(copy.start)
                else:
                    copy.start()

    def send_key_grads(h, xk, d):
        remote(
            dkv.at[h, xk, d], rkv.at[h, x, k], dks.at[h, xk, d], dkr.at[h, x, k],
            place(z, a, d, xk, b),
        ).start()

    def add_passed(h, xk, d):
        done(rel.at[h, d], rlr.at[h, d])
        for which in range(2):
            for j in range(5):
                dkv[h, xk, d, which, j] += rel[h, d, which, j]

    def send_query_grads(h):
        for dy, dk in ((1, 0), (1, 1), (0, 1)):
            d = (k + dk) % 2
            to = (b + dy) % 2
            remote(
                dqb.at[h, to, d], rdq.at[h, b, k], dqs.at[h, dy, dk], dqr.at[h, b, k],
                place(z, a, d, x, to),
            ).start()

    alive = jnp.broadcast_to(m_ref[pl.ds(row, 1), :], (128, 128)).astype(F32).T
    alive = jnp.concatenate([alive, alive], axis=1) == 1.0
    for h in range(4):
        sbb[h % 2, h // 2] = jnp.where(alive, b_ref[h] * LOG2E, -1e30)
    for d in range(2):
        for h in range(2):
            slr[d, 0, h] = l_ref[:, 2 * d + h, :]
            slr[d, 1, h] = r_ref[:, 2 * d + h, :]

    pl.semaphore_wait(barrier, len(partners))

    send_bias(0)
    turn(k_ref, skv, 0)
    turn(v_ref, skv, 1)
    send_keys(0)
    pltpu.make_async_copy(slr.at[k], lrb.at[b, k], lrr.at[b, k]).start()
    for dy, dk in ((1, 0), (1, 1), (0, 1)):
        d = (k + dk) % 2
        remote(
            slr.at[d], lrb.at[b, k], lrs.at[dy, dk], lrr.at[b, k], place(z, a, d, x, (b + dy) % 2)
        ).start()
    turn(q_ref, sqg, 0)
    turn(g_ref, sqg, 1)
    share_queries(0)
    send_queries(0)
    share_queries(1)
    spread_bias(0)
    pass_keys(0)
    send_keys(1)
    pass_bias(0)
    wait_levels(b)
    take_queries(0, b)
    take_queries(1, b)
    wait_levels(1 - b)
    take_queries(0, 1 - b)
    send_bias(1)

    def block_of(t):
        return (x + 2 + 3 * t + 3 * (t // 2) + 2 * (t // 3)) % 4

    def block(n, carry):
        h = n // 4
        t = n % 4
        xk = block_of(t)

        @pl.when(n == 4)
        def _():
            take_queries(1, 1 - b)

        wait_keys(h, xk)
        wait_bias(h, xk)
        compute_block(
            kvb.at[h, xk], qp.at[h], gp.at[h], bb.at[h, xk], dkv.at[h, xk], dqb.at[h],
            dbb.at[h, xk], scr, t == 0,
        )
        send_bias_grad(h, xk)
        pl.when(t == 3)(lambda: send_query_grads(h))

        @pl.when(t == 0)
        def _():
            for d, dx in ((0, 1), (1, 3)):
                remote(
                    dkv.at[h, xk, d], rel.at[h, d], rls.at[h, d], rlr.at[h, d], at(dx=dx)
                ).start()

        @pl.when(t == 1)
        def _():
            send_key_grads(h, right, 1)

        @pl.when(t == 2)
        def _():
            add_passed(h, right, 0)
            send_key_grads(h, right, 0)
            send_key_grads(h, left, 0)

        @pl.when(t == 3)
        def _():
            send_key_grads(h, x, 1 - k)
            add_passed(h, left, 1)
            send_key_grads(h, left, 1)

        @pl.when(n > 0)
        def _():
            finish_bias_grad((n - 1) // 4, block_of((n - 1) % 4))

        @pl.when(n == 0)
        def _():
            spread_bias(1)
            send_queries(1)

        @pl.when(n == 1)
        def _():
            pass_keys(1)

        @pl.when(n == 2)
        def _():
            pass_bias(1)

        @pl.when(n == 6)
        def _():
            sum_bias(0)

        return carry

    lax.fori_loop(0, 8, block, 0)
    finish_bias_grad(1, x)

    for h in range(2):
        done(rkv.at[h, x, 1 - k], dkr.at[h, x, 1 - k])
        for xk in (right, left):
            for c in range(2):
                done(rkv.at[h, xk, c], dkr.at[h, xk, c])

    def join(own, other):
        low = jnp.where(k == 0, own, other)
        high = jnp.where(k == 0, other, own)
        return jnp.concatenate([low, high], axis=0).T

    def rows(ref, *index):
        return jnp.concatenate([ref[(0, *index)], ref[(1, *index)]], axis=0)

    for j in range(5):
        for which, out in ((0, dk_ref), (1, dv_ref)):
            own = rows(dkv, x, k, which, j)
            other = rows(rkv, x, 1 - k, which, j)
            for xk in (right, left):
                own = own + rows(rkv, xk, k, which, j)
                other = other + rows(rkv, xk, 1 - k, which, j)
            out[j] = join(own, other)
    sum_bias(1)
    for h in range(2):
        for dy, dk in ((1, 0), (1, 1), (0, 1)):
            done(rdq.at[h, (b + dy) % 2, (k + dk) % 2], dqr.at[h, (b + dy) % 2, (k + dk) % 2])
    for j in range(5):
        own = rows(dqb, b, k, j) + rows(rdq, 1 - b, k, j)
        other = rows(rdq, 0, 1 - k, j) + rows(rdq, 1, 1 - k, j)
        dq_ref[j] = join(own, other)
    for h in range(2):
        for half in range(2):
            for part in range(2):
                done(rbb.at[h, half, part], d1r.at[h, half, part])
        for d in range(2):
            db_ref[2 * d + h] = rbb[h, 0, d] + rbb[h, 1, d]

    for h in range(2):
        for i in range(7):
            done(skv.at[0, 0], kvs.at[h, i])
        done(dkv.at[0, 0, 0], dks.at[h, x, 1 - k])
        for d in range(2):
            done(dkv.at[0, 0, 0], dks.at[h, right, d])
            done(dkv.at[0, 0, 0], dks.at[h, left, d])
            done(rel.at[0, 0], rls.at[h, d])
        for dy, dk in ((1, 0), (1, 1), (0, 1)):
            done(sqg.at[0, 0], qgs.at[h, dy, dk])
            done(dqb.at[0, 0, 0], dqs.at[h, dy, dk])
            done(sbb.at[0, 0], b1s.at[h, dy, dk])
            done(sbb.at[0, 0], d1s.at[h, dy, dk])
        for i in range(6):
            done(bb.at[0, 0, 0], b2s.at[h, i])
        for to in range(2):
            done(zrel.at[0, 0], zls.at[h, to])
            for half in range(2):
                done(zrel.at[0, 0], dbs.at[h, to, half])
    for dy, dk in ((1, 0), (1, 1), (0, 1)):
        done(slr.at[0], lrs.at[dy, dk])

    @pl.when(a != b)
    def _():
        for h in range(2):
            done(sbb.at[0, 0], b1s.at[h, 0, 0])
            done(sbb.at[0, 0], d1s.at[h, 0, 0])


def hand_over(*refs):
    for i in range(4):
        refs[4 + i][...] = refs[i][...]


def body(query_proj, key_proj, value_proj, out_grad, pair_bias, log_sum_exp, correction, pad_mask):
    vmem = pl.BlockSpec(memory_space=pltpu.VMEM)
    f = lambda *shape: pltpu.VMEM(shape, F32)
    dma = lambda *shape: pltpu.SemaphoreType.DMA(shape)
    swap = lambda y: jnp.transpose(y, (1, 0, 2))
    pair = [dma(2, 2, 2)] * 2
    dq, dk, dv, db = pl.pallas_call(
        kernel,
        out_shape=[jax.ShapeDtypeStruct((5, 256, 128), F32)] * 3
        + [jax.ShapeDtypeStruct((4, 128, 256), F32)],
        in_specs=[vmem] * 8,
        out_specs=[vmem] * 4,
        scratch_shapes=[
            f(2, 2, 2, 5, 32, 256),
            f(2, 2, 2, 5, 32, 256),
            f(2, 2, 128, 256),
            f(2, 2, 2, 5, 256),
            f(2, 4, 2, 2, 5, 32, 256),
            f(2, 2, 2, 2, 5, 32, 256),
            f(2, 2, 2, 2, 5, 256),
            f(2, 4, 2, 2, 128, 256),
            f(2, 4, 2, 2, 5, 32, 256),
            f(2, 4, 2, 2, 5, 32, 256),
            f(2, 2, 2, 5, 32, 256),
            f(2, 2, 2, 128, 256),
            f(2, 2, 2, 5, 32, 256),
            f(2, 2, 2, 5, 32, 256),
            f(2, 4, 2, 2, 128, 256),
            f(2, 2, 2, 2, 128, 256),
            f(2, 2, 2, 128, 256),
            pltpu.VMEM((2, 2, 5, 128, 512), BF),
            pltpu.VMEM((2, 2, 5, 128, 512), BF),
            pltpu.VMEM((4, 4, 256, 512), BF),
            dma(2, 7), dma(2, 4, 2), *pair, dma(2, 2), dma(2, 2), *pair, dma(2, 6), dma(2, 4, 2),
            dma(2, 4, 2), dma(2, 4, 2), dma(2, 2), dma(2, 2), *pair, dma(2, 2), dma(2, 2), dma(2, 2, 2), dma(2, 2, 2), *pair,
        ],
        compiler_params=pltpu.CompilerParams(
            collective_id=0, has_side_effects=True, vmem_limit_bytes=60 * 2**20
        ),
    )(
        swap(query_proj), swap(key_proj), swap(value_proj), swap(out_grad), pair_bias,
        swap(log_sum_exp), swap(correction), pad_mask.reshape(16, 128),
    )
    flat = lambda y: y.reshape(1280, 128)
    rows = pl.BlockSpec((320, 128), lambda i: (i, 0))
    plane = pl.BlockSpec((1, 128, 256), lambda i: (i, 0, 0))
    dq, dk, dv, db = pl.pallas_call(
        hand_over,
        grid=(4,),
        out_shape=[jax.ShapeDtypeStruct((1280, 128), F32)] * 3
        + [jax.ShapeDtypeStruct((4, 128, 256), F32)],
        in_specs=[rows] * 3 + [plane],
        out_specs=[rows] * 3 + [plane],
    )(flat(dq), flat(dk), flat(dv), db)
    whole = lambda y: swap(y.reshape(5, 256, 128))
    return whole(dq), whole(dk), whole(dv), db


def solution(mesh):
    return jax.shard_map(
        body,
        mesh=mesh,
        in_specs=(
            P("col", "row", None),
            P("col", "row", None),
            P("col", "row", None),
            P("col", "row", None),
            P(None, "row", "col"),
            P(None, "row", "col"),
            P(None, "row", "col"),
            P(),
        ),
        out_specs=(
            P("col", "row", None),
            P("col", "row", None),
            P("col", "row", None),
            P(None, "row", "col"),
        ),
        check_vma=False,
    )
```
